256 devices in a mesh: row: 32 (over z, y_hi, core), col: 8 (over x, y_lo).
Axes of the slice: x: 4, y: 4 (y_hi: 2, y_lo: 2; y = y_hi * 2 + y_lo), z: 8, core: 2. Of those that a mesh axis runs over, the one named last changes fastest.
Arguments:
- vectors_in: float32 [1024, 196608], P(('col', 'row')), may hold values from -6 to 6
- householder: float32 [4, 64, 196608], P(None, None, 'row'), may hold values from -0.013671875 to 0.013671875
- tfactors: float32 [4, 64, 64], replicated, as said below
Outputs:
- vectors_out: float32 [1024, 196608], P('col', 'row')
The draws below stay inside these ranges and needn't reach their ends.
Inputs may be any that keep to these rules, and one draw needn't show every extreme that they name: `tfactors`: every factor is upper triangular with its diagonal between 1 and 2.
All inputs are finite; a program needn't handle non-finite values.
Results may differ from the reference program's by a relative error of at most 0.0001.
Values sent between devices are 32-bit elements; how exact they have to be, the bound alone decides.
No kernel may reach another device: no remote copies, remote signals or barrier semaphores. Data moves between devices by JAX's collectives and lax.ppermute only.
A program may use at most 64 MiB of HBM per device.

```python
import jax
import jax.numpy as jnp
from jax import lax

K = 1024
HB = 64
PANELS = 4
NROWS = 196608


def draw_tfactors(key, part):
    key = jax.random.fold_in(key, 7)
    key_diag, key_off = jax.random.split(key)
    diag_part = jax.random.uniform(key_diag, (PANELS, HB), jnp.float32, 1.0, 2.0)
    off_part = 0.25 * jax.random.normal(key_off, (PANELS, HB, HB), jnp.float32)
    upper = jnp.triu(off_part, 1)
    eye_mat = jnp.eye(HB, dtype=jnp.float32)
    return upper + diag_part[:, :, None] * eye_mat[None, :, :]


def shard_levels(own_key, shape, cuts, low, largest):
    level = 1.0
    for position, shards_of in cuts:
        steps = jax.random.uniform(jax.random.fold_in(jax.random.fold_in(own_key, 6), position), (shards_of,), jnp.float32, low / len(cuts), largest / len(cuts))
        level = level * jnp.repeat(jnp.exp(steps), shape[position] // shards_of).reshape((-1,) + (1,) * (len(shape) - 1 - position))
    return level


def centred(rng, shape, width, limit, shards=(), held_as=jnp.bfloat16):
    values = jax.random.normal(rng, shape, jnp.float32) * width
    if len(shards) > 0:
        values = shard_levels(rng, shape, shards, -0.22, 0.18) * values
    return jnp.clip(values, min=-limit, max=limit).astype(held_as)


def setup_inputs(seed: int = 0) -> dict:
    seeds = jax.random.split(jax.random.key(seed), 4)
    vectors_in = centred(seeds[0], (K, NROWS), 1.0, 6.0, ((0, 256),), jnp.float32)
    householder = centred(seeds[1], (PANELS, HB, NROWS), NROWS ** -0.5, 0.013671875, ((2, 32),), jnp.float32)
    tfactors = draw_tfactors(jax.random.fold_in(seeds[3], 71), 0)
    return dict(vectors_in=vectors_in, householder=householder, tfactors=tfactors)


def reference(vectors_in, householder, tfactors):
    current = vectors_in
    for index in range(PANELS - 1, -1, -1):
        basis = householder[index]
        proj = jnp.dot(current, basis.T, precision=lax.Precision.HIGHEST, preferred_element_type=jnp.float32)
        scaled = jnp.dot(proj, tfactors[index].T, precision=lax.Precision.HIGHEST, preferred_element_type=jnp.float32)
        current = current - jnp.dot(scaled, basis, precision=lax.Precision.HIGHEST, preferred_element_type=jnp.float32)
    return current
```

```python
import jax
import jax.numpy as jnp
from jax import lax
from jax.sharding import PartitionSpec as P


def product(left, right, contract, precision=lax.Precision.HIGHEST):
    return lax.dot_general(
        left,
        right,
        ((contract[:1], contract[1:]), ((), ())),
        precision=precision,
        preferred_element_type=jnp.float32,
    )


def swap(value, bit, devices):
    return lax.ppermute(value, "row", [(i, i ^ bit) for i in range(devices)])


def halves(value, upper):
    half = value.shape[0] // 2
    parts = value.reshape(2, half, value.shape[1])
    return parts[upper], parts[1 - upper]


def whole_sum(value, devices):
    index = lax.axis_index("row")
    for bit in (1, 2):
        kept, sent = halves(value, (index // bit) % 2)
        value = kept + swap(sent, bit, devices)
    bit = 4
    while bit < devices:
        value = value + swap(value, bit, devices)
        bit *= 2
    for bit in (2, 1):
        other = swap(value, bit, devices)
        upper = (index // bit) % 2 == 1
        value = jnp.concatenate([jnp.where(upper, other, value), jnp.where(upper, value, other)], axis=0)
    return value


def solution(mesh):
    devices = mesh.shape["row"]

    def shards(vectors_in, householder, tfactors):
        panels, width, rows = householder.shape
        basis = householder.reshape(panels * width, rows)
        gram = product(basis, basis, (1, 1))
        current = lax.all_to_all(vectors_in, "row", split_axis=1, concat_axis=0, tiled=True)
        count = current.shape[0]
        proj = product(current, basis, (1, 1))
        total = whole_sum(jnp.concatenate([proj, gram], axis=0), devices)
        proj, gram = total[:count], total[count:]
        scaled = [None] * panels
        for p in range(panels - 1, -1, -1):
            own = proj[:, p * width : (p + 1) * width]
            for q in range(p + 1, panels):
                block = gram[p * width : (p + 1) * width, q * width : (q + 1) * width]
                own = own - product(scaled[q], block, (1, 1))
            scaled[p] = product(own, tfactors[p], (1, 1))
        scaled = jnp.concatenate(scaled, axis=1)
        return current - product(scaled, basis, (1, 0))

    in_specs = (P(("col", "row"), None), P(None, None, "row"), P())
    out_specs = P("col", "row")
    return jax.shard_map(shards, mesh=mesh, in_specs=in_specs, out_specs=out_specs, check_vma=False)
```

```python
import functools

import jax
import jax.numpy as jnp
from jax import lax
from jax.experimental import pallas as pl
from jax.experimental.pallas import tpu as pltpu
from jax.sharding import PartitionSpec as P

COLUMNS = 1024
LIMIT = 40 * 1024 * 1024
IN_VMEM = pl.BlockSpec(memory_space=pltpu.VMEM)
IN_SMEM = pl.BlockSpec(memory_space=pltpu.SMEM)
IN_HBM = pl.BlockSpec(memory_space=pl.ANY)


def product(left, right, contract, precision=None):
    return lax.dot_general(
        left, right, (contract, ((), ())), precision=precision, preferred_element_type=jnp.float32
    )


def split(value):
    high = value.astype(jnp.bfloat16)
    low = (value - high.astype(jnp.float32)).astype(jnp.bfloat16)
    return high, low


def pairs_of(panels):
    return [(p, q) for p in range(panels) for q in range(p + 1, panels)]


def gram_kernel(householder_ref, basis_ref, gram_ref, total):
    panels, width, rows = householder_ref.shape
    size = panels * width
    total[...] = jnp.zeros_like(total)

    @pl.loop(0, rows // COLUMNS)
    def _(step):
        columns = pl.ds(pl.multiple_of(step * COLUMNS, COLUMNS), COLUMNS)
        block = householder_ref[:, :, columns].reshape(size, COLUMNS)
        high, low = split(block)
        basis_ref[:size, columns] = high
        basis_ref[size:, columns] = low
        total[...] += product(block, block, ((1,), (1,)), lax.Precision.HIGHEST)

    blocks = [
        total[p * width : (p + 1) * width, q * width : (q + 1) * width] for p, q in pairs_of(panels)
    ]
    for i in range(0, len(blocks), 2):
        at = i // 2 * width
        gram_ref[at : at + width, :] = jnp.concatenate(blocks[i : i + 2], axis=1)


def project_kernel(quarter_ref, arrived_ref, basis_ref, gram_ref, current_ref, kept_ref, sent_ref, total, joint):
    count, rows = current_ref.shape
    size = basis_ref.shape[0] // 2
    total[...] = jnp.zeros_like(total)
    for step in range(rows // COLUMNS):
        columns = pl.ds(step * COLUMNS, COLUMNS)
        block = arrived_ref[:, :, columns].reshape(count, COLUMNS)
        current_ref[:, columns] = block
        high, low = split(block)
        both = jnp.concatenate([high, low], axis=0)
        total[...] += product(basis_ref[:, columns], both, ((1,), (1,)))
    joint[:size, :] = (total[:size, :count] + total[:size, count:]) + (total[size:, :count] + total[size:, count:])
    joint[size:, :] = gram_ref[...]
    quarter = quarter_ref[0]
    part = joint.shape[0] // 4
    for k in range(4):
        target = (kept_ref, sent_ref, kept_ref, sent_ref)[k]
        start = pl.multiple_of((quarter ^ k) * part, 8)
        target[k // 2 * part : (k // 2 + 1) * part, :] = joint[pl.ds(start, part), :]


def finish_kernel(quarter_ref, own_ref, across_ref, other_ref, tfactors_ref, current_ref, basis_ref, out_ref, joint, out, sems):
    panels, width, _ = tfactors_ref.shape
    count, rows = current_ref.shape
    size = panels * width
    quarter = quarter_ref[0]
    part = joint.shape[0] // 4
    parts = (own_ref[...], other_ref[:part, :], across_ref[...], other_ref[part:, :])
    for k in range(4):
        joint[pl.ds(pl.multiple_of((quarter ^ k) * part, 8), part), :] = parts[k]
    gram = {}
    for i, pair in enumerate(pairs_of(panels)):
        at = size + i // 2 * width
        gram[pair] = joint[at : at + width, i % 2 * width : (i % 2 + 1) * width]
    exact = functools.partial(product, contract=((1,), (0,)), precision=lax.Precision.HIGHEST)
    scaled = [exact(tfactors_ref[p], joint[p * width : (p + 1) * width, :]) for p in range(panels)]
    links = {(p, q): exact(tfactors_ref[p], gram[p, q]) for p, q in gram}
    for q in range(panels - 1, 0, -1):
        for p in range(q):
            scaled[p] = scaled[p] - exact(links[p, q], scaled[q])
    high, low = split(jnp.concatenate(scaled, axis=0).T)
    both = jnp.concatenate([high, low], axis=0)
    copies = []
    for step in range(rows // COLUMNS):
        columns = pl.ds(step * COLUMNS, COLUMNS)
        first = product(both, basis_ref[:size, columns], ((1,), (0,)))
        second = product(high, basis_ref[size:, columns], ((1,), (0,)))
        out[:, columns] = current_ref[:, columns] - (first[:count] + (first[count:] + second))
        copy = pltpu.make_async_copy(out.at[:, columns], out_ref.at[:, columns], sems.at[step])
        copy.start()
        copies.append(copy)
    for copy in copies:
        copy.wait()


def in_vmem(value):
    return pltpu.with_memory_space_constraint(value, pltpu.VMEM)


def gram_call(householder):
    panels, width, rows = householder.shape
    size = panels * width
    pairs = len(pairs_of(panels))
    return pl.pallas_call(
        gram_kernel,
        out_shape=(
            pltpu.VMEM((2 * size, rows), jnp.bfloat16),
            jax.ShapeDtypeStruct((pairs // 2 * width, 2 * width), jnp.float32),
        ),
        in_specs=[IN_VMEM],
        out_specs=(IN_VMEM, IN_VMEM),
        scratch_shapes=[pltpu.VMEM((size, size), jnp.float32)],
        compiler_params=pltpu.CompilerParams(vmem_limit_bytes=LIMIT),
        cost_estimate=pl.CostEstimate(flops=12 * size * size * rows, bytes_accessed=4 * size * rows, transcendentals=0),
        name="gram",
    )(householder)


def project_call(quarter, arrived, basis, gram):
    sources, each, rows = arrived.shape
    count = sources * each
    size = basis.shape[0] // 2
    height = size + gram.shape[0]
    return pl.pallas_call(
        project_kernel,
        out_shape=(
            pltpu.VMEM((count, rows), jnp.float32),
            pltpu.VMEM((height // 2, count), jnp.float32),
            pltpu.VMEM((height // 2, count), jnp.float32),
        ),
        in_specs=[IN_SMEM, IN_VMEM, IN_VMEM, IN_VMEM],
        out_specs=(IN_VMEM, IN_VMEM, IN_VMEM),
        scratch_shapes=[
            pltpu.VMEM((2 * size, 2 * count), jnp.float32),
            pltpu.VMEM((height, count), jnp.float32),
        ],
        compiler_params=pltpu.CompilerParams(vmem_limit_bytes=LIMIT),
        name="project",
    )(quarter, in_vmem(arrived), in_vmem(basis), gram)


def finish_call(quarter, own, across, other, tfactors, current, basis):
    count, rows = current.shape
    return pl.pallas_call(
        finish_kernel,
        out_shape=jax.ShapeDtypeStruct((count, rows), jnp.float32),
        in_specs=[IN_SMEM] + [IN_VMEM] * 6,
        out_specs=IN_HBM,
        scratch_shapes=[
            pltpu.VMEM((4 * own.shape[0], count), jnp.float32),
            pltpu.VMEM((count, rows), jnp.float32),
            pltpu.SemaphoreType.DMA((rows // COLUMNS,)),
        ],
        compiler_params=pltpu.CompilerParams(vmem_limit_bytes=LIMIT),
        name="finish",
    )(quarter, in_vmem(own), in_vmem(across), in_vmem(other), tfactors, in_vmem(current), in_vmem(basis))


def solution(mesh):
    devices = mesh.shape["row"]

    def swap(value, flip):
        return lax.ppermute(value, "row", [(i, i ^ flip) for i in range(devices)])

    def shards(vectors_in, householder, tfactors):
        quarter = jnp.reshape(lax.axis_index("row") % 4, (1,)).astype(jnp.int32)
        arrived = lax.all_to_all(
            vectors_in.reshape(vectors_in.shape[0], devices, -1), "row", split_axis=1, concat_axis=0
        )
        basis, gram = gram_call(householder)
        current, kept, sent = project_call(quarter, arrived, basis, gram)
        part = kept.shape[0] // 2
        kept = kept + swap(sent, 1)
        value = kept[:part] + swap(kept[part:], 2)
        flip = 4
        while flip < devices:
            value = value + swap(value, 2 * flip - 4)
            flip *= 2
        across = swap(value, 2)
        other = swap(jnp.concatenate([value, across], axis=0), 1)
        return finish_call(quarter, value, across, other, tfactors, current, basis)

    in_specs = (P(("col", "row"), None), P(None, None, "row"), P())
    out_specs = P("col", "row")
    return jax.shard_map(shards, mesh=mesh, in_specs=in_specs, out_specs=out_specs, check_vma=False)
```

```python
import functools

import jax
import jax.numpy as jnp
from jax import lax
from jax.experimental import pallas as pl
from jax.experimental.pallas import tpu as pltpu
from jax.sharding import Mesh
from jax.sharding import PartitionSpec as P

COLUMNS = 1024
LIMIT = 40 * 1024 * 1024
IN_VMEM = pl.BlockSpec(memory_space=pltpu.VMEM)
IN_SMEM = pl.BlockSpec(memory_space=pltpu.SMEM)
IN_HBM = pl.BlockSpec(memory_space=pl.ANY)


def product(left, right, contract, precision=None):
    return lax.dot_general(
        left, right, (contract, ((), ())), precision=precision, preferred_element_type=jnp.float32
    )


def split(value):
    high = value.astype(jnp.bfloat16)
    low = (value - high.astype(jnp.float32)).astype(jnp.bfloat16)
    return high, low


def pairs_of(panels):
    return [(p, q) for p in range(panels) for q in range(p + 1, panels)]


def gram_kernel(householder_ref, basis_ref, gram_ref, total):
    panels, width, columns = householder_ref.shape
    size = panels * width
    step = pl.program_id(0)

    @pl.when(step == 0)
    def _():
        total[...] = jnp.zeros_like(total)

    high, low = split(householder_ref[...].reshape(size, columns))
    both = jnp.concatenate([high, low], axis=0)
    basis_ref[...] = both
    first = product(both, high, ((1,), (1,)))
    second = product(both, low, ((1,), (1,)))
    total[...] += (first[:size] + first[size:]) + (second[:size] + second[size:])

    @pl.when(step == pl.num_programs(0) - 1)
    def _():
        blocks = [
            total[p * width : (p + 1) * width, q * width : (q + 1) * width] for p, q in pairs_of(panels)
        ]
        for i in range(0, len(blocks), 2):
            at = i // 2 * width
            gram_ref[at : at + width, :] = jnp.concatenate(blocks[i : i + 2], axis=1)


def project_kernel(core_ref, arrived_ref, basis_ref, current_ref, held_ref, kept_ref, sent_ref, total, joint, sems):
    count, rows = current_ref.shape
    size = basis_ref.shape[0] // 2
    copies = []
    for step in range(rows // COLUMNS):
        columns = pl.ds(step * COLUMNS, COLUMNS)
        copy = pltpu.make_async_copy(basis_ref.at[:, columns], held_ref.at[:, columns], sems.at[step])
        copy.start()
        copies.append(copy)
    total[...] = jnp.zeros_like(total)
    for step in range(rows // COLUMNS):
        columns = pl.ds(step * COLUMNS, COLUMNS)
        block = arrived_ref[:, :, columns].reshape(count, COLUMNS)
        current_ref[:, columns] = block
        high, low = split(block)
        both = jnp.concatenate([high, low], axis=0)
        copies[step].wait()
        total[...] += product(held_ref[:, columns], both, ((1,), (1,)))
    joint[...] = (total[:size, :count] + total[:size, count:]) + (total[size:, :count] + total[size:, count:])
    core = core_ref[0]
    half = size // 2
    kept_ref[...] = joint[pl.ds(pl.multiple_of(core * half, 8), half), :]
    sent_ref[...] = joint[pl.ds(pl.multiple_of((1 - core) * half, 8), half), :]


def finish_kernel(core_ref, own_ref, other_ref, gram_ref, tfactors_ref, current_ref, basis_ref, out_ref, joint, out, sems):
    panels, width, _ = tfactors_ref.shape
    count, rows = current_ref.shape
    size = panels * width
    core = core_ref[0]
    half = size // 2
    joint[pl.ds(pl.multiple_of(core * half, 8), half), :] = own_ref[...]
    joint[pl.ds(pl.multiple_of((1 - core) * half, 8), half), :] = other_ref[...]
    gram = {}
    for i, pair in enumerate(pairs_of(panels)):
        at = i // 2 * width
        gram[pair] = gram_ref[at : at + width, i % 2 * width : (i % 2 + 1) * width]
    exact = functools.partial(product, contract=((1,), (0,)), precision=lax.Precision.HIGHEST)
    scaled = [exact(tfactors_ref[p], joint[p * width : (p + 1) * width, :]) for p in range(panels)]
    links = {(p, q): exact(tfactors_ref[p], gram[p, q]) for p, q in gram}
    for q in range(panels - 1, 0, -1):
        for p in range(q):
            scaled[p] = scaled[p] - exact(links[p, q], scaled[q])
    high, low = split(jnp.concatenate(scaled, axis=0).T)
    both = jnp.concatenate([high, low], axis=0)
    copies = []
    for step in range(rows // COLUMNS):
        columns = pl.ds(step * COLUMNS, COLUMNS)
        first = product(both, basis_ref[:size, columns], ((1,), (0,)))
        second = product(high, basis_ref[size:, columns], ((1,), (0,)))
        out[:, columns] = current_ref[:, columns] - (first[:count] + (first[count:] + second))
        copy = pltpu.make_async_copy(out.at[:, columns], out_ref.at[:, columns], sems.at[step])
        copy.start()
        copies.append(copy)
    for copy in copies:
        copy.wait()


def in_vmem(value):
    return pltpu.with_memory_space_constraint(value, pltpu.VMEM)


def in_hbm(value):
    return pltpu.with_memory_space_constraint(value, pltpu.HBM)


def gram_call(householder):
    panels, width, rows = householder.shape
    size = panels * width
    height = len(pairs_of(panels)) // 2 * width
    return pl.pallas_call(
        gram_kernel,
        out_shape=(
            pltpu.HBM((2 * size, rows), jnp.bfloat16),
            jax.ShapeDtypeStruct((height, 2 * width), jnp.float32),
        ),
        grid=(rows // COLUMNS,),
        in_specs=[pl.BlockSpec((panels, width, COLUMNS), lambda i: (0, 0, i))],
        out_specs=(
            pl.BlockSpec((2 * size, COLUMNS), lambda i: (0, i)),
            pl.BlockSpec((height, 2 * width), lambda i: (0, 0)),
        ),
        scratch_shapes=[pltpu.VMEM((size, size), jnp.float32)],
        compiler_params=pltpu.CompilerParams(vmem_limit_bytes=LIMIT),
        cost_estimate=pl.CostEstimate(flops=8 * size * size * rows, bytes_accessed=8 * size * rows, transcendentals=0),
        name="gram",
    )(in_hbm(householder))


def project_call(core, arrived, basis):
    sources, each, rows = arrived.shape
    count = sources * each
    size = basis.shape[0] // 2
    return pl.pallas_call(
        project_kernel,
        out_shape=(
            pltpu.VMEM((count, rows), jnp.float32),
            pltpu.VMEM((2 * size, rows), jnp.bfloat16),
            pltpu.VMEM((size // 2, count), jnp.float32),
            pltpu.VMEM((size // 2, count), jnp.float32),
        ),
        in_specs=[IN_SMEM, IN_VMEM, pl.BlockSpec(memory_space=pltpu.HBM)],
        out_specs=(IN_VMEM, IN_VMEM, IN_VMEM, IN_VMEM),
        scratch_shapes=[
            pltpu.VMEM((2 * size, 2 * count), jnp.float32),
            pltpu.VMEM((size, count), jnp.float32),
            pltpu.SemaphoreType.DMA((rows // COLUMNS,)),
        ],
        compiler_params=pltpu.CompilerParams(vmem_limit_bytes=LIMIT),
        name="project",
    )(core, in_vmem(arrived), in_hbm(basis))


def finish_call(core, own, other, gram, tfactors, current, basis):
    count, rows = current.shape
    return pl.pallas_call(
        finish_kernel,
        out_shape=jax.ShapeDtypeStruct((count, rows), jnp.float32),
        in_specs=[IN_SMEM] + [IN_VMEM] * 6,
        out_specs=IN_HBM,
        scratch_shapes=[
            pltpu.VMEM((2 * own.shape[0], count), jnp.float32),
            pltpu.VMEM((count, rows), jnp.float32),
            pltpu.SemaphoreType.DMA((rows // COLUMNS,)),
        ],
        compiler_params=pltpu.CompilerParams(vmem_limit_bytes=LIMIT),
        name="finish",
    )(core, in_vmem(own), in_vmem(other), gram, tfactors, in_vmem(current), in_vmem(basis))


def solution(mesh):
    devices, columns = mesh.shape["row"], mesh.shape["col"]
    planes = devices // 4
    row = ("z", "y", "core")
    parts = Mesh(mesh.devices.reshape(planes, 2, 2, columns), row + ("col",))

    def swap(value, flip):
        return lax.ppermute(value, row, [(i, i ^ flip) for i in range(devices)])

    def shards(vectors_in, householder, tfactors):
        core = jnp.reshape(lax.axis_index("core"), (1,)).astype(jnp.int32)
        arrived = lax.all_to_all(
            vectors_in.reshape(vectors_in.shape[0], devices, -1), row, split_axis=1, concat_axis=0
        )
        basis, gram = gram_call(householder)
        gram = gram + swap(gram, 1)
        gram = gram + swap(gram, 2)
        gram = lax.psum(gram, "z")
        current, held, kept, sent = project_call(core, arrived, basis)
        value = kept + swap(sent, 1)
        value = value + swap(value, 2)
        first, second, third = swap(value, 4), swap(value, 8), swap(value, 12)
        value = (value + first) + (second + third)
        value = value + swap(value, 24)
        other = swap(value, 1)
        return finish_call(core, value, other, gram, tfactors, current, held)

    in_specs = (P(("col",) + row, None), P(None, None, row), P())
    out_specs = P("col", row)
    return jax.shard_map(shards, mesh=parts, in_specs=in_specs, out_specs=out_specs, check_vma=False)
```

```python
import functools

import jax
import jax.numpy as jnp
from jax import lax
from jax.experimental import pallas as pl
from jax.experimental.pallas import tpu as pltpu
from jax.sharding import PartitionSpec as P

COLUMNS = 1024
LIMIT = 40 * 1024 * 1024
IN_VMEM = pl.BlockSpec(memory_space=pltpu.VMEM)
IN_SMEM = pl.BlockSpec(memory_space=pltpu.SMEM)
IN_HBM = pl.BlockSpec(memory_space=pl.ANY)


def product(left, right, contract, precision=None):
    return lax.dot_general(
        left, right, (contract, ((), ())), precision=precision, preferred_element_type=jnp.float32
    )


def split(value):
    high = value.astype(jnp.bfloat16)
    low = (value - high.astype(jnp.float32)).astype(jnp.bfloat16)
    return high, low


def pairs_of(panels):
    return [(p, q) for p in range(panels) for q in range(p + 1, panels)]


def halves(core, whole, own_ref, other_ref):
    half = whole.shape[0] // 2
    own_ref[...] = whole[pl.ds(pl.multiple_of(core * half, 8), half), :]
    other_ref[...] = whole[pl.ds(pl.multiple_of((1 - core) * half, 8), half), :]


def gram_kernel(core_ref, householder_ref, high_ref, low_ref, kept_ref, sent_ref, total, packed):
    panels, width, columns = householder_ref.shape
    size = panels * width
    step = pl.program_id(0)

    @pl.when(step == 0)
    def _():
        total[...] = jnp.zeros_like(total)

    high, low = split(householder_ref[...].reshape(size, columns))
    high_ref[...] = high
    low_ref[...] = low
    both = jnp.concatenate([high, low], axis=0)
    first = product(both, high, ((1,), (1,)))
    second = product(both, low, ((1,), (1,)))
    total[...] += (first[:size] + first[size:]) + (second[:size] + second[size:])

    @pl.when(step == pl.num_programs(0) - 1)
    def _():
        blocks = [
            total[p * width : (p + 1) * width, q * width : (q + 1) * width] for p, q in pairs_of(panels)
        ]
        for i in range(0, len(blocks), 2):
            at = i // 2 * width
            packed[at : at + width, :] = jnp.concatenate(blocks[i : i + 2], axis=1)
        halves(core_ref[0], packed, kept_ref, sent_ref)


def project_high_kernel(arrived_ref, high_ref, current_ref, rounded_ref, total_ref):
    count, rows = current_ref.shape
    total_ref[...] = jnp.zeros_like(total_ref)
    for step in range(rows // COLUMNS):
        columns = pl.ds(step * COLUMNS, COLUMNS)
        block = arrived_ref[:, :, columns].reshape(count, COLUMNS)
        current_ref[:, columns] = block
        high, low = split(block)
        rounded_ref[:, columns] = high
        both = jnp.concatenate([high, low], axis=0)
        total_ref[...] += product(high_ref[:, columns], both, ((1,), (1,)))


def project_low_kernel(core_ref, total_ref, rounded_ref, low_ref, before_ref, kept_ref, sent_ref, whole):
    del before_ref
    count = rounded_ref.shape[0]
    whole[...] = total_ref[:, :count] + (
        total_ref[:, count:] + product(low_ref[...], rounded_ref[...], ((1,), (1,)))
    )
    halves(core_ref[0], whole, kept_ref, sent_ref)


def finish_kernel(core_ref, own_ref, other_ref, tfactors_ref, current_ref, high_ref, low_ref, out_ref, joint, packed, out, sems):
    panels, width, _ = tfactors_ref.shape
    count, rows = current_ref.shape
    core = core_ref[0]
    half, rest = joint.shape[0] // 2, packed.shape[0] // 2
    for side, part_ref in ((core, own_ref), (1 - core, other_ref)):
        joint[pl.ds(pl.multiple_of(side * half, 8), half), :] = part_ref[:half, :]
        packed[pl.ds(pl.multiple_of(side * rest, 8), rest), :] = part_ref[half:, :]
    gram = {}
    for i, pair in enumerate(pairs_of(panels)):
        at = i // 2 * width
        gram[pair] = packed[at : at + width, i % 2 * width : (i % 2 + 1) * width]
    exact = functools.partial(product, contract=((1,), (0,)), precision=lax.Precision.HIGHEST)
    scaled = [exact(tfactors_ref[p], joint[p * width : (p + 1) * width, :]) for p in range(panels)]
    links = {(p, q): exact(tfactors_ref[p], gram[p, q]) for p, q in gram}
    for q in range(panels - 1, 0, -1):
        for p in range(q):
            scaled[p] = scaled[p] - exact(links[p, q], scaled[q])
    high, low = split(jnp.concatenate(scaled, axis=0).T)
    both = jnp.concatenate([high, low], axis=0)
    copies = []
    for step in range(rows // COLUMNS):
        columns = pl.ds(step * COLUMNS, COLUMNS)
        first = product(both, high_ref[:, columns], ((1,), (0,)))
        second = product(high, low_ref[:, columns], ((1,), (0,)))
        out[:, columns] = current_ref[:, columns] - (first[:count] + (first[count:] + second))
        copy = pltpu.make_async_copy(out.at[:, columns], out_ref.at[:, columns], sems.at[step])
        copy.start()
        copies.append(copy)
    for copy in copies:
        copy.wait()


def in_vmem(value):
    return pltpu.with_memory_space_constraint(value, pltpu.VMEM)


def in_hbm(value):
    return pltpu.with_memory_space_constraint(value, pltpu.HBM)


def gram_call(core, householder):
    panels, width, rows = householder.shape
    size = panels * width
    height = len(pairs_of(panels)) // 2 * width
    return pl.pallas_call(
        gram_kernel,
        out_shape=(
            pltpu.HBM((size, rows), jnp.bfloat16),
            pltpu.HBM((size, rows), jnp.bfloat16),
            jax.ShapeDtypeStruct((height // 2, 2 * width), jnp.float32),
            jax.ShapeDtypeStruct((height // 2, 2 * width), jnp.float32),
        ),
        grid=(rows // COLUMNS,),
        in_specs=[IN_SMEM, pl.BlockSpec((panels, width, COLUMNS), lambda i: (0, 0, i))],
        out_specs=(
            pl.BlockSpec((size, COLUMNS), lambda i: (0, i)),
            pl.BlockSpec((size, COLUMNS), lambda i: (0, i)),
            pl.BlockSpec((height // 2, 2 * width), lambda i: (0, 0)),
            pl.BlockSpec((height // 2, 2 * width), lambda i: (0, 0)),
        ),
        scratch_shapes=[pltpu.VMEM((size, size), jnp.float32), pltpu.VMEM((height, 2 * width), jnp.float32)],
        compiler_params=pltpu.CompilerParams(vmem_limit_bytes=LIMIT),
        cost_estimate=pl.CostEstimate(flops=8 * size * size * rows, bytes_accessed=8 * size * rows, transcendentals=0),
        name="gram",
    )(core, in_hbm(householder))


def project_call(core, arrived, high, low, before):
    sources, each, rows = arrived.shape
    count = sources * each
    size = high.shape[0]
    current, rounded, total = pl.pallas_call(
        project_high_kernel,
        out_shape=(
            pltpu.VMEM((count, rows), jnp.float32),
            pltpu.VMEM((count, rows), jnp.bfloat16),
            pltpu.VMEM((size, 2 * count), jnp.float32),
        ),
        in_specs=[IN_VMEM, IN_VMEM],
        out_specs=(IN_VMEM, IN_VMEM, IN_VMEM),
        compiler_params=pltpu.CompilerParams(vmem_limit_bytes=LIMIT),
        name="project_high",
    )(in_vmem(arrived), in_vmem(high))
    kept, sent = pl.pallas_call(
        project_low_kernel,
        out_shape=(
            pltpu.VMEM((size // 2, count), jnp.float32),
            pltpu.VMEM((size // 2, count), jnp.float32),
        ),
        in_specs=[IN_SMEM, IN_VMEM, IN_VMEM, IN_VMEM, IN_HBM],
        out_specs=(IN_VMEM, IN_VMEM),
        scratch_shapes=[pltpu.VMEM((size, count), jnp.float32)],
        compiler_params=pltpu.CompilerParams(vmem_limit_bytes=LIMIT),
        name="project_low",
    )(core, in_vmem(total), in_vmem(rounded), in_vmem(low), before)
    return current, kept, sent


def finish_call(core, own, other, tfactors, current, high, low):
    count, rows = current.shape
    size = high.shape[0]
    return pl.pallas_call(
        finish_kernel,
        out_shape=jax.ShapeDtypeStruct((count, rows), jnp.float32),
        in_specs=[IN_SMEM] + [IN_VMEM] * 6,
        out_specs=IN_HBM,
        scratch_shapes=[
            pltpu.VMEM((size, count), jnp.float32),
            pltpu.VMEM((2 * own.shape[0] - size, count), jnp.float32),
            pltpu.VMEM((count, rows), jnp.float32),
            pltpu.SemaphoreType.DMA((rows // COLUMNS,)),
        ],
        compiler_params=pltpu.CompilerParams(vmem_limit_bytes=LIMIT),
        name="finish",
    )(core, in_vmem(own), in_vmem(other), tfactors, in_vmem(current), in_vmem(high), in_vmem(low))


def solution(mesh):
    devices = mesh.shape["row"]

    def swap(value, flip):
        return lax.ppermute(value, "row", [(i, i ^ flip) for i in range(devices)])

    def shards(vectors_in, householder, tfactors):
        core = jnp.reshape(lax.axis_index("row") % 2, (1,)).astype(jnp.int32)
        arrived = lax.all_to_all(
            vectors_in.reshape(vectors_in.shape[0], devices, -1), "row", split_axis=1, concat_axis=0
        )
        high, low, gram, sent = gram_call(core, householder)
        gram = gram + swap(sent, 1)
        gram = gram + swap(gram, 2)
        gram = gram + swap(gram, 4)
        current, value, sent = project_call(core, arrived, high, low, gram)
        value = value + swap(sent, 1)
        across = swap(value, 2)
        gram = gram + swap(gram, 24)
        value = value + across
        first, third = swap(value, 4), swap(value, 12)
        second = swap(jnp.concatenate([value, gram], axis=0), 8)
        half = value.shape[0]
        value = (value + first) + (second[:half] + third)
        gram = gram + second[half:]
        value = value + swap(value, 24)
        own = jnp.concatenate([value, gram], axis=0)
        other = swap(own, 1)
        return finish_call(core, own, other, tfactors, current, high, low)

    in_specs = (P(("col", "row"), None), P(None, None, "row"), P())
    out_specs = P("col", "row")
    return jax.shard_map(shards, mesh=mesh, in_specs=in_specs, out_specs=out_specs, check_vma=False)
```

```python
import functools

import jax
import jax.numpy as jnp
from jax import lax
from jax.experimental import pallas as pl
from jax.experimental.pallas import tpu as pltpu
from jax.sharding import PartitionSpec as P

COLUMNS = 1024
OUT_COLUMNS = 2048
LIMIT = 40 * 1024 * 1024
IN_VMEM = pl.BlockSpec(memory_space=pltpu.VMEM)
IN_SMEM = pl.BlockSpec(memory_space=pltpu.SMEM)
IN_HBM = pl.BlockSpec(memory_space=pl.ANY)


def product(left, right, contract, precision=None):
    return lax.dot_general(
        left, right, (contract, ((), ())), precision=precision, preferred_element_type=jnp.float32
    )


def split(value):
    high = value.astype(jnp.bfloat16)
    low = (value - high.astype(jnp.float32)).astype(jnp.bfloat16)
    return high, low


def pairs_of(panels):
    return [(p, q) for p in range(panels) for q in range(p + 1, panels)]


def halves(core, whole, own_ref, other_ref):
    half = whole.shape[0] // 2
    own_ref[...] = whole[pl.ds(pl.multiple_of(core * half, 8), half), :]
    other_ref[...] = whole[pl.ds(pl.multiple_of((1 - core) * half, 8), half), :]


def gram_kernel(core_ref, householder_ref, high_ref, low_ref, kept_ref, sent_ref, total, packed):
    panels, width, columns = householder_ref.shape
    size = panels * width
    step = pl.program_id(0)

    @pl.when(step == 0)
    def _():
        total[...] = jnp.zeros_like(total)

    high, low = split(householder_ref[...].reshape(size, columns))
    high_ref[...] = high
    low_ref[...] = low
    both = jnp.concatenate([high, low], axis=0)
    first = product(both, high, ((1,), (1,)))
    second = product(both, low, ((1,), (1,)))
    total[...] += (first[:size] + first[size:]) + (second[:size] + second[size:])

    @pl.when(step == pl.num_programs(0) - 1)
    def _():
        blocks = [
            total[p * width : (p + 1) * width, q * width : (q + 1) * width] for p, q in pairs_of(panels)
        ]
        for i in range(0, len(blocks), 2):
            at = i // 2 * width
            packed[at : at + width, :] = jnp.concatenate(blocks[i : i + 2], axis=1)
        halves(core_ref[0], packed, kept_ref, sent_ref)


def project_high_kernel(arrived_ref, high_ref, current_ref, rounded_ref, total_ref):
    count, rows = current_ref.shape
    total_ref[...] = jnp.zeros_like(total_ref)
    for step in range(rows // COLUMNS):
        columns = pl.ds(step * COLUMNS, COLUMNS)
        block = arrived_ref[:, :, columns].reshape(count, COLUMNS)
        current_ref[:, columns] = block
        high, low = split(block)
        rounded_ref[:, columns] = high
        both = jnp.concatenate([high, low], axis=0)
        total_ref[...] += product(high_ref[:, columns], both, ((1,), (1,)))


def project_low_kernel(core_ref, total_ref, rounded_ref, low_ref, gram_ref, more_ref, kept_ref, sent_ref, sum_ref, whole):
    sum_ref[...] = gram_ref[...] + more_ref[...]
    count = rounded_ref.shape[0]
    whole[...] = total_ref[:, :count] + (
        total_ref[:, count:] + product(low_ref[...], rounded_ref[...], ((1,), (1,)))
    )
    halves(core_ref[0], whole, kept_ref, sent_ref)


def finish_kernel(core_ref, own_ref, other_ref, tfactors_ref, current_ref, high_ref, low_ref, out_ref, joint, packed, out, sems):
    panels, width, _ = tfactors_ref.shape
    count, rows = current_ref.shape
    core = core_ref[0]
    half, rest = joint.shape[0] // 2, packed.shape[0] // 2
    for side, part_ref in ((core, own_ref), (1 - core, other_ref)):
        joint[pl.ds(pl.multiple_of(side * half, 8), half), :] = part_ref[:half, :]
        packed[pl.ds(pl.multiple_of(side * rest, 8), rest), :] = part_ref[half:, :]
    gram = {}
    for i, pair in enumerate(pairs_of(panels)):
        at = i // 2 * width
        gram[pair] = packed[at : at + width, i % 2 * width : (i % 2 + 1) * width]
    exact = functools.partial(product, contract=((1,), (0,)), precision=lax.Precision.HIGHEST)
    scaled = [exact(tfactors_ref[p], joint[p * width : (p + 1) * width, :]) for p in range(panels)]
    links = {(p, q): exact(tfactors_ref[p], gram[p, q]) for p, q in gram}
    for q in range(panels - 1, 0, -1):
        for p in range(q):
            scaled[p] = scaled[p] - exact(links[p, q], scaled[q])
    high, low = split(jnp.concatenate(scaled, axis=0).T)
    both = jnp.concatenate([high, low], axis=0)
    copies = []
    for step in range(rows // OUT_COLUMNS):
        columns = pl.ds(step * OUT_COLUMNS, OUT_COLUMNS)
        first = product(both, high_ref[:, columns], ((1,), (0,)))
        second = product(high, low_ref[:, columns], ((1,), (0,)))
        out[:, columns] = current_ref[:, columns] - (first[:count] + (first[count:] + second))
        copy = pltpu.make_async_copy(out.at[:, columns], out_ref.at[:, columns], sems.at[step])
        copy.start()
        copies.append(copy)
    for copy in copies:
        copy.wait()


def in_vmem(value):
    return pltpu.with_memory_space_constraint(value, pltpu.VMEM)


def in_hbm(value):
    return pltpu.with_memory_space_constraint(value, pltpu.HBM)


def gram_call(core, householder):
    panels, width, rows = householder.shape
    size = panels * width
    height = len(pairs_of(panels)) // 2 * width
    return pl.pallas_call(
        gram_kernel,
        out_shape=(
            pltpu.HBM((size, rows), jnp.bfloat16),
            pltpu.HBM((size, rows), jnp.bfloat16),
            jax.ShapeDtypeStruct((height // 2, 2 * width), jnp.float32),
            jax.ShapeDtypeStruct((height // 2, 2 * width), jnp.float32),
        ),
        grid=(rows // COLUMNS,),
        in_specs=[IN_SMEM, pl.BlockSpec((panels, width, COLUMNS), lambda i: (0, 0, i))],
        out_specs=(
            pl.BlockSpec((size, COLUMNS), lambda i: (0, i)),
            pl.BlockSpec((size, COLUMNS), lambda i: (0, i)),
            pl.BlockSpec((height // 2, 2 * width), lambda i: (0, 0)),
            pl.BlockSpec((height // 2, 2 * width), lambda i: (0, 0)),
        ),
        scratch_shapes=[pltpu.VMEM((size, size), jnp.float32), pltpu.VMEM((height, 2 * width), jnp.float32)],
        compiler_params=pltpu.CompilerParams(vmem_limit_bytes=LIMIT),
        cost_estimate=pl.CostEstimate(flops=8 * size * size * rows, bytes_accessed=8 * size * rows, transcendentals=0),
        name="gram",
    )(core, in_hbm(householder))


def project_call(core, arrived, high, low, gram, more):
    sources, each, rows = arrived.shape
    count = sources * each
    size = high.shape[0]
    current, rounded, total = pl.pallas_call(
        project_high_kernel,
        out_shape=(
            pltpu.VMEM((count, rows), jnp.float32),
            pltpu.VMEM((count, rows), jnp.bfloat16),
            pltpu.VMEM((size, 2 * count), jnp.float32),
        ),
        in_specs=[IN_VMEM, IN_VMEM],
        out_specs=(IN_VMEM, IN_VMEM, IN_VMEM),
        compiler_params=pltpu.CompilerParams(vmem_limit_bytes=LIMIT),
        name="project_high",
    )(in_vmem(arrived), in_vmem(high))
    kept, sent, gram = pl.pallas_call(
        project_low_kernel,
        out_shape=(
            pltpu.VMEM((size // 2, count), jnp.float32),
            pltpu.VMEM((size // 2, count), jnp.float32),
            pltpu.VMEM(gram.shape, jnp.float32),
        ),
        in_specs=[IN_SMEM] + [IN_VMEM] * 5,
        out_specs=(IN_VMEM, IN_VMEM, IN_VMEM),
        scratch_shapes=[pltpu.VMEM((size, count), jnp.float32)],
        compiler_params=pltpu.CompilerParams(vmem_limit_bytes=LIMIT),
        name="project_low",
    )(core, in_vmem(total), in_vmem(rounded), in_vmem(low), in_vmem(gram), in_vmem(more))
    return current, kept, sent, gram


def finish_call(core, own, other, tfactors, current, high, low):
    count, rows = current.shape
    size = high.shape[0]
    return pl.pallas_call(
        finish_kernel,
        out_shape=jax.ShapeDtypeStruct((count, rows), jnp.float32),
        in_specs=[IN_SMEM] + [IN_VMEM] * 6,
        out_specs=IN_HBM,
        scratch_shapes=[
            pltpu.VMEM((size, count), jnp.float32),
            pltpu.VMEM((2 * own.shape[0] - size, count), jnp.float32),
            pltpu.VMEM((count, rows), jnp.float32),
            pltpu.SemaphoreType.DMA((rows // OUT_COLUMNS,)),
        ],
        compiler_params=pltpu.CompilerParams(vmem_limit_bytes=LIMIT),
        name="finish",
    )(core, in_vmem(own), in_vmem(other), tfactors, in_vmem(current), in_vmem(high), in_vmem(low))


def solution(mesh):
    devices = mesh.shape["row"]

    def swap(value, flip):
        return lax.ppermute(value, "row", [(i, i ^ flip) for i in range(devices)])

    def shards(vectors_in, householder, tfactors):
        core = jnp.reshape(lax.axis_index("row") % 2, (1,)).astype(jnp.int32)
        arrived = lax.all_to_all(
            vectors_in.reshape(vectors_in.shape[0], devices, -1), "row", split_axis=1, concat_axis=0
        )
        high, low, gram, sent = gram_call(core, householder)
        gram = gram + swap(sent, 1)
        gram = gram + swap(gram, 2)
        gram = gram + swap(gram, 4)
        current, value, sent, gram = project_call(core, arrived, high, low, gram, swap(gram, 24))
        value = value + swap(sent, 1)
        value = value + swap(value, 2)
        first, third = swap(value, 4), swap(value, 12)
        second = swap(jnp.concatenate([value, gram], axis=0), 8)
        half = value.shape[0]
        value = (value + first) + (second[:half] + third)
        gram = gram + second[half:]
        value = value + swap(value, 24)
        own = jnp.concatenate([value, gram], axis=0)
        other = swap(own, 1)
        return finish_call(core, own, other, tfactors, current, high, low)

    in_specs = (P(("col", "row"), None), P(None, None, "row"), P())
    out_specs = P("col", "row")
    return jax.shard_map(shards, mesh=mesh, in_specs=in_specs, out_specs=out_specs, check_vma=False)
```

```python
import functools

import jax
import jax.numpy as jnp
from jax import lax
from jax.experimental import pallas as pl
from jax.experimental.pallas import tpu as pltpu
from jax.sharding import Mesh
from jax.sharding import PartitionSpec as P

COLUMNS = 1024
OUT_COLUMNS = 2048
SHIFTS = (1, -1, 3, -3)
LIMIT = 40 * 1024 * 1024
IN_VMEM = pl.BlockSpec(memory_space=pltpu.VMEM)
IN_SMEM = pl.BlockSpec(memory_space=pltpu.SMEM)
IN_ANY = pl.BlockSpec(memory_space=pl.ANY)
IN_HBM = pl.BlockSpec(memory_space=pltpu.HBM)


def product(left, right, contract, precision=None):
    return lax.dot_general(
        left, right, (contract, ((), ())), precision=precision, preferred_element_type=jnp.float32
    )


def split(value):
    high = value.astype(jnp.bfloat16)
    low = (value - high.astype(jnp.float32)).astype(jnp.bfloat16)
    return high, low


def pairs_of(panels):
    return [(p, q) for p in range(panels) for q in range(p + 1, panels)]


def halves(core, whole, own_ref, other_ref):
    half = whole.shape[0] // 2
    own_ref[...] = whole[pl.ds(pl.multiple_of(core * half, 8), half), :]
    other_ref[...] = whole[pl.ds(pl.multiple_of((1 - core) * half, 8), half), :]


def gram_kernel(core_ref, householder_ref, before_ref, high_ref, low_ref, kept_ref, sent_ref, total, packed):
    del before_ref
    panels, width, columns = householder_ref.shape
    size = panels * width
    step = pl.program_id(0)

    @pl.when(step == 0)
    def _():
        total[...] = jnp.zeros_like(total)

    high, low = split(householder_ref[...].reshape(size, columns))
    high_ref[...] = high
    low_ref[...] = low
    both = jnp.concatenate([high, low], axis=0)
    first = product(both, high, ((1,), (1,)))
    second = product(both, low, ((1,), (1,)))
    total[...] += (first[:size] + first[size:]) + (second[:size] + second[size:])

    @pl.when(step == pl.num_programs(0) - 1)
    def _():
        blocks = [
            total[p * width : (p + 1) * width, q * width : (q + 1) * width] for p, q in pairs_of(panels)
        ]
        for i in range(0, len(blocks), 2):
            at = i // 2 * width
            packed[at : at + width, :] = jnp.concatenate(blocks[i : i + 2], axis=1)
        halves(core_ref[0], packed, kept_ref, sent_ref)


def cut_kernel(place_ref, vectors_ref, *refs):
    outs, sems = refs[:-1], refs[-1]
    wide = outs[0].shape[1]
    planes = vectors_ref.shape[1] // wide
    copies = []
    for i, shift in enumerate(SHIFTS):
        plane = (place_ref[0] + shift + planes) % planes
        columns = pl.ds(pl.multiple_of(plane * wide, 128), wide)
        copies.append(pltpu.make_async_copy(vectors_ref.at[:, columns], outs[i], sems.at[i]))
        copies[i].start()
    for copy in copies:
        copy.wait()


def even_kernel(place_ref, vectors_ref, before_ref, out_ref, sems):
    del before_ref
    number, _, wide = out_ref.shape
    copies = []
    for i in range(number):
        block = (i // 4 * 2 + place_ref[0] % 2) * 4 + i % 4
        columns = pl.ds(pl.multiple_of(block * wide, 128), wide)
        copies.append(pltpu.make_async_copy(vectors_ref.at[:, columns], out_ref.at[i], sems.at[i]))
        copies[i].start()
    for copy in copies:
        copy.wait()


def side_kernel(place_ref, up_ref, down_ref, before_ref, kept_ref, sent_ref):
    del before_ref
    wide = kept_ref.shape[2]
    y = place_ref[1]
    for i, part_ref in enumerate((up_ref, down_ref)):
        kept_ref[i] = part_ref[:, pl.ds(pl.multiple_of(y * wide, 128), wide)]
        sent_ref[i] = part_ref[:, pl.ds(pl.multiple_of((1 - y) * wide, 128), wide)]


def core_kernel(place_ref, own_ref, got_ref, kept_ref, sent_ref):
    wide = kept_ref.shape[3]
    core = place_ref[2]
    for i, part_ref in enumerate((own_ref, got_ref)):
        kept_ref[i] = part_ref[:, :, pl.ds(pl.multiple_of(core * wide, 128), wide)]
        sent_ref[i] = part_ref[:, :, pl.ds(pl.multiple_of((1 - core) * wide, 128), wide)]


def project_high_kernel(place_ref, even_ref, kept_one_ref, got_one_ref, kept_three_ref, got_three_ref, high_ref, current_ref, rounded_ref, total_ref):
    count, rows = current_ref.shape
    planes = count // (4 * even_ref.shape[1])
    z, y, core = place_ref[0], place_ref[1], place_ref[2]
    pair = 2 * even_ref.shape[1]
    total_ref[...] = jnp.zeros_like(total_ref)
    for step in range(rows // COLUMNS):
        columns = pl.ds(step * COLUMNS, COLUMNS)

        def put(plane, side, block):
            at = pl.multiple_of((plane * 2 + side) * pair, 8)
            current_ref[pl.ds(at, pair), columns] = block

        for k in range(planes // 2):
            for side in range(2):
                at = (2 * k + side) * 2
                put(2 * k + z % 2, side, even_ref[at : at + 2, :, columns].reshape(pair, COLUMNS))
        for shift, kept_ref, got_ref in ((1, kept_one_ref, got_one_ref), (3, kept_three_ref, got_three_ref)):
            for other in range(2):
                for i, by in enumerate((shift, -shift)):
                    kept, got = kept_ref[other, i, :, columns], got_ref[other, i, :, columns]
                    block = jnp.concatenate([jnp.where(core == 0, kept, got), jnp.where(core == 0, got, kept)], axis=0)
                    put((z - by + planes) % planes, y ^ other, block)
        high, low = split(current_ref[:, columns])
        rounded_ref[:, columns] = high
        both = jnp.concatenate([high, low], axis=0)
        total_ref[...] += product(high_ref[:, columns], both, ((1,), (1,)))


def project_low_kernel(core_ref, total_ref, rounded_ref, low_ref, gram_ref, more_ref, kept_ref, sent_ref, sum_ref, whole):
    sum_ref[...] = gram_ref[...] + more_ref[...]
    count = rounded_ref.shape[0]
    whole[...] = total_ref[:, :count] + (
        total_ref[:, count:] + product(low_ref[...], rounded_ref[...], ((1,), (1,)))
    )
    halves(core_ref[0], whole, kept_ref, sent_ref)


def finish_kernel(core_ref, own_ref, other_ref, tfactors_ref, current_ref, high_ref, low_ref, out_ref, joint, packed, out, sems):
    panels, width, _ = tfactors_ref.shape
    count, rows = current_ref.shape
    core = core_ref[0]
    half, rest = joint.shape[0] // 2, packed.shape[0] // 2
    for side, part_ref in ((core, own_ref), (1 - core, other_ref)):
        joint[pl.ds(pl.multiple_of(side * half, 8), half), :] = part_ref[:half, :]
        packed[pl.ds(pl.multiple_of(side * rest, 8), rest), :] = part_ref[half:, :]
    gram = {}
    for i, pair in enumerate(pairs_of(panels)):
        at = i // 2 * width
        gram[pair] = packed[at : at + width, i % 2 * width : (i % 2 + 1) * width]
    exact = functools.partial(product, contract=((1,), (0,)), precision=lax.Precision.HIGHEST)
    scaled = [exact(tfactors_ref[p], joint[p * width : (p + 1) * width, :]) for p in range(panels)]
    links = {(p, q): exact(tfactors_ref[p], gram[p, q]) for p, q in gram}
    for q in range(panels - 1, 0, -1):
        for p in range(q):
            scaled[p] = scaled[p] - exact(links[p, q], scaled[q])
    high, low = split(jnp.concatenate(scaled, axis=0).T)
    both = jnp.concatenate([high, low], axis=0)
    copies = []
    for step in range(rows // OUT_COLUMNS):
        columns = pl.ds(step * OUT_COLUMNS, OUT_COLUMNS)
        first = product(both, high_ref[:, columns], ((1,), (0,)))
        second = product(high, low_ref[:, columns], ((1,), (0,)))
        out[:, columns] = current_ref[:, columns] - (first[:count] + (first[count:] + second))
        copy = pltpu.make_async_copy(out.at[:, columns], out_ref.at[:, columns], sems.at[step])
        copy.start()
        copies.append(copy)
    for copy in copies:
        copy.wait()


def in_vmem(value):
    return pltpu.with_memory_space_constraint(value, pltpu.VMEM)


def in_hbm(value):
    return pltpu.with_memory_space_constraint(value, pltpu.HBM)


def gram_call(core, householder, before):
    panels, width, rows = householder.shape
    size = panels * width
    height = len(pairs_of(panels)) // 2 * width
    return pl.pallas_call(
        gram_kernel,
        out_shape=(
            pltpu.HBM((size, rows), jnp.bfloat16),
            pltpu.HBM((size, rows), jnp.bfloat16),
            jax.ShapeDtypeStruct((height // 2, 2 * width), jnp.float32),
            jax.ShapeDtypeStruct((height // 2, 2 * width), jnp.float32),
        ),
        grid=(rows // COLUMNS,),
        in_specs=[IN_SMEM, pl.BlockSpec((panels, width, COLUMNS), lambda i: (0, 0, i)), IN_ANY],
        out_specs=(
            pl.BlockSpec((size, COLUMNS), lambda i: (0, i)),
            pl.BlockSpec((size, COLUMNS), lambda i: (0, i)),
            pl.BlockSpec((height // 2, 2 * width), lambda i: (0, 0)),
            pl.BlockSpec((height // 2, 2 * width), lambda i: (0, 0)),
        ),
        scratch_shapes=[pltpu.VMEM((size, size), jnp.float32), pltpu.VMEM((height, 2 * width), jnp.float32)],
        compiler_params=pltpu.CompilerParams(vmem_limit_bytes=LIMIT),
        cost_estimate=pl.CostEstimate(flops=10 * 8 * size * size * rows, bytes_accessed=8 * size * rows, transcendentals=0),
        name="gram",
    )(core, in_hbm(householder), before)


def local_call(kernel, outs, specs, operands, copies=0):
    return pl.pallas_call(
        kernel,
        out_shape=outs,
        in_specs=[IN_SMEM] + specs,
        out_specs=tuple(IN_HBM if out.memory_space == pltpu.HBM else IN_VMEM for out in outs),
        scratch_shapes=[pltpu.SemaphoreType.DMA((copies,))] if copies else [],
        compiler_params=pltpu.CompilerParams(vmem_limit_bytes=LIMIT),
        name=kernel.__name__,
    )(*operands)


def project_call(core, place, even, odd, high, low, gram, more):
    sources, each, rows = even.shape
    count = 2 * sources * each
    size = high.shape[0]
    current, rounded, total = pl.pallas_call(
        project_high_kernel,
        out_shape=(
            pltpu.VMEM((count, rows), jnp.float32),
            pltpu.VMEM((count, rows), jnp.bfloat16),
            pltpu.VMEM((size, 2 * count), jnp.float32),
        ),
        in_specs=[IN_SMEM] + [IN_VMEM] * 6,
        out_specs=(IN_VMEM, IN_VMEM, IN_VMEM),
        compiler_params=pltpu.CompilerParams(vmem_limit_bytes=LIMIT),
        name="project_high",
    )(place, in_vmem(even), *[in_vmem(part) for part in odd], in_vmem(high))
    kept, sent, gram = pl.pallas_call(
        project_low_kernel,
        out_shape=(
            pltpu.VMEM((size // 2, count), jnp.float32),
            pltpu.VMEM((size // 2, count), jnp.float32),
            pltpu.VMEM(gram.shape, jnp.float32),
        ),
        in_specs=[IN_SMEM] + [IN_VMEM] * 5,
        out_specs=(IN_VMEM, IN_VMEM, IN_VMEM),
        scratch_shapes=[pltpu.VMEM((size, count), jnp.float32)],
        compiler_params=pltpu.CompilerParams(vmem_limit_bytes=LIMIT),
        name="project_low",
    )(core, in_vmem(total), in_vmem(rounded), in_vmem(low), in_vmem(gram), in_vmem(more))
    return current, kept, sent, gram


def finish_call(core, own, other, tfactors, current, high, low):
    count, rows = current.shape
    size = high.shape[0]
    return pl.pallas_call(
        finish_kernel,
        out_shape=jax.ShapeDtypeStruct((count, rows), jnp.float32),
        in_specs=[IN_SMEM] + [IN_VMEM] * 6,
        out_specs=IN_ANY,
        scratch_shapes=[
            pltpu.VMEM((size, count), jnp.float32),
            pltpu.VMEM((2 * own.shape[0] - size, count), jnp.float32),
            pltpu.VMEM((count, rows), jnp.float32),
            pltpu.SemaphoreType.DMA((rows // OUT_COLUMNS,)),
        ],
        compiler_params=pltpu.CompilerParams(vmem_limit_bytes=LIMIT),
        name="finish",
    )(core, in_vmem(own), in_vmem(other), tfactors, in_vmem(current), in_vmem(high), in_vmem(low))


def solution(mesh):
    devices, columns = mesh.shape["row"], mesh.shape["col"]
    planes = devices // 4
    row = ("half", "odd", "y", "core")
    parts = Mesh(mesh.devices.reshape(planes // 2, 2, 2, 2, columns), row + ("col",))

    def swap(value, flip):
        return lax.ppermute(value, row, [(i, i ^ flip) for i in range(devices)])

    def shards(vectors_in, householder, tfactors):
        odd, y, core = lax.axis_index("odd"), lax.axis_index("y"), lax.axis_index("core")
        z = lax.axis_index("half") * 2 + odd
        place = jnp.stack([z, y, core]).astype(jnp.int32)
        core = jnp.reshape(core, (1,)).astype(jnp.int32)
        each, length = vectors_in.shape
        wide = length // planes

        def moved(part, shift):
            return lax.ppermute(part, ("half", "odd"), [(i, (i + shift) % planes) for i in range(planes)])

        def spread(up, down, before):
            block = pltpu.VMEM((2, each, wide // 2), jnp.float32)
            kept, sent = local_call(side_kernel, (block, block), [IN_VMEM, IN_VMEM, IN_ANY], (place, up, down, before))
            block = pltpu.VMEM((2, 2, each, wide // 4), jnp.float32)
            kept, sent = local_call(core_kernel, (block, block), [IN_VMEM, IN_VMEM], (place, kept, swap(sent, 2)))
            return kept, swap(sent, 1)

        block = pltpu.VMEM((each, wide), jnp.float32)
        cut = local_call(cut_kernel, (block,) * len(SHIFTS), [IN_HBM], (place, in_hbm(vectors_in)), len(SHIFTS))
        came = [moved(part, shift) for part, shift in zip(cut, SHIFTS)]
        block = pltpu.HBM((devices // 2, each, wide // 4), jnp.float32)
        (even,) = local_call(even_kernel, (block,), [IN_HBM, IN_ANY], (place, in_hbm(vectors_in), came[0]), devices // 2)
        even = lax.all_to_all(even, ("half", "y", "core"), split_axis=0, concat_axis=0, tiled=True)
        high, low, gram, sent = gram_call(core, householder, came[0])
        scattered = spread(came[0], came[1], came[0]) + spread(came[2], came[3], gram)
        gram = gram + swap(sent, 1)
        gram = gram + swap(gram, 2)
        gram = gram + swap(gram, 4)
        current, value, sent, gram = project_call(core, place, even, scattered, high, low, gram, swap(gram, 24))
        value = value + swap(sent, 1)
        value = value + swap(value, 2)
        first, third = swap(value, 4), swap(value, 12)
        second = swap(jnp.concatenate([value, gram], axis=0), 8)
        half = value.shape[0]
        value = (value + first) + (second[:half] + third)
        gram = gram + second[half:]
        value = value + swap(value, 24)
        own = jnp.concatenate([value, gram], axis=0)
        other = swap(own, 1)
        return finish_call(core, own, other, tfactors, current, high, low)

    in_specs = (P(("col",) + row, None), P(None, None, row), P())
    out_specs = P("col", row)
    return jax.shard_map(shards, mesh=parts, in_specs=in_specs, out_specs=out_specs, check_vma=False)
```

```python
import functools

import jax
import jax.numpy as jnp
from jax import lax
from jax.experimental import pallas as pl
from jax.experimental.pallas import tpu as pltpu
from jax.sharding import Mesh
from jax.sharding import PartitionSpec as P

COLUMNS = 1024
OUT_COLUMNS = 2048
SHIFTS = (1, -1, 3, -3)
LIMIT = 40 * 1024 * 1024
IN_VMEM = pl.BlockSpec(memory_space=pltpu.VMEM)
IN_SMEM = pl.BlockSpec(memory_space=pltpu.SMEM)
IN_ANY = pl.BlockSpec(memory_space=pl.ANY)
IN_HBM = pl.BlockSpec(memory_space=pltpu.HBM)


def product(left, right, contract, precision=None):
    return lax.dot_general(
        left, right, (contract, ((), ())), precision=precision, preferred_element_type=jnp.float32
    )


def split(value):
    high = value.astype(jnp.bfloat16)
    low = (value - high.astype(jnp.float32)).astype(jnp.bfloat16)
    return high, low


def pairs_of(panels):
    return [(p, q) for p in range(panels) for q in range(p + 1, panels)]


def halves(core, whole, own_ref, other_ref):
    half = whole.shape[0] // 2
    own_ref[...] = whole[pl.ds(pl.multiple_of(core * half, 8), half), :]
    other_ref[...] = whole[pl.ds(pl.multiple_of((1 - core) * half, 8), half), :]


def gram_kernel(core_ref, householder_ref, high_ref, low_ref, kept_ref, sent_ref, total, packed):
    panels, width, columns = householder_ref.shape
    size = panels * width
    step = pl.program_id(0)

    @pl.when(step == 0)
    def _():
        total[...] = jnp.zeros_like(total)

    high, low = split(householder_ref[...].reshape(size, columns))
    high_ref[...] = high
    low_ref[...] = low
    both = jnp.concatenate([high, low], axis=0)
    first = product(both, high, ((1,), (1,)))
    second = product(both, low, ((1,), (1,)))
    total[...] += (first[:size] + first[size:]) + (second[:size] + second[size:])

    @pl.when(step == pl.num_programs(0) - 1)
    def _():
        blocks = [
            total[p * width : (p + 1) * width, q * width : (q + 1) * width] for p, q in pairs_of(panels)
        ]
        for i in range(0, len(blocks), 2):
            at = i // 2 * width
            packed[at : at + width, :] = jnp.concatenate(blocks[i : i + 2], axis=1)
        halves(core_ref[0], packed, kept_ref, sent_ref)


def cut_kernel(place_ref, vectors_ref, *refs):
    outs, sems = refs[:-1], refs[-1]
    wide = outs[0].shape[1]
    planes = vectors_ref.shape[1] // wide
    copies = []
    for i, shift in enumerate(SHIFTS):
        plane = (place_ref[0] + shift + planes) % planes
        columns = pl.ds(pl.multiple_of(plane * wide, 128), wide)
        copies.append(pltpu.make_async_copy(vectors_ref.at[:, columns], outs[i], sems.at[i]))
        copies[i].start()
    for copy in copies:
        copy.wait()


def even_kernel(place_ref, block_ref, out_ref):
    del place_ref
    number, _, wide = out_ref.shape
    for i in range(number):
        out_ref[i] = block_ref[:, i * wide : (i + 1) * wide]


def side_kernel(place_ref, up_ref, down_ref, before_ref, kept_ref, sent_ref):
    del before_ref
    wide = kept_ref.shape[2]
    y = place_ref[1]
    for i, part_ref in enumerate((up_ref, down_ref)):
        kept_ref[i] = part_ref[:, pl.ds(pl.multiple_of(y * wide, 128), wide)]
        sent_ref[i] = part_ref[:, pl.ds(pl.multiple_of((1 - y) * wide, 128), wide)]


def core_kernel(place_ref, own_ref, got_ref, kept_ref, sent_ref):
    wide = kept_ref.shape[3]
    core = place_ref[2]
    for i, part_ref in enumerate((own_ref, got_ref)):
        kept_ref[i] = part_ref[:, :, pl.ds(pl.multiple_of(core * wide, 128), wide)]
        sent_ref[i] = part_ref[:, :, pl.ds(pl.multiple_of((1 - core) * wide, 128), wide)]


def project_high_kernel(place_ref, even_ref, kept_one_ref, got_one_ref, kept_three_ref, got_three_ref, high_ref, current_ref, rounded_ref, total_ref):
    count, rows = current_ref.shape
    planes = count // (4 * even_ref.shape[1])
    z, y, core = place_ref[0], place_ref[1], place_ref[2]
    pair = 2 * even_ref.shape[1]
    total_ref[...] = jnp.zeros_like(total_ref)
    for step in range(rows // COLUMNS):
        columns = pl.ds(step * COLUMNS, COLUMNS)

        def put(plane, side, block):
            at = pl.multiple_of((plane * 2 + side) * pair, 8)
            current_ref[pl.ds(at, pair), columns] = block

        for k in range(planes // 2):
            for side in range(2):
                at = (2 * k + side) * 2
                put(2 * k + z % 2, side, even_ref[at : at + 2, :, columns].reshape(pair, COLUMNS))
        for shift, kept_ref, got_ref in ((1, kept_one_ref, got_one_ref), (3, kept_three_ref, got_three_ref)):
            for other in range(2):
                for i, by in enumerate((shift, -shift)):
                    kept, got = kept_ref[other, i, :, columns], got_ref[other, i, :, columns]
                    block = jnp.concatenate([jnp.where(core == 0, kept, got), jnp.where(core == 0, got, kept)], axis=0)
                    put((z - by + planes) % planes, y ^ other, block)
        high, low = split(current_ref[:, columns])
        rounded_ref[:, columns] = high
        both = jnp.concatenate([high, low], axis=0)
        total_ref[...] += product(high_ref[:, columns], both, ((1,), (1,)))


def project_low_kernel(core_ref, total_ref, rounded_ref, low_ref, gram_ref, more_ref, kept_ref, sent_ref, sum_ref, whole):
    sum_ref[...] = gram_ref[...] + more_ref[...]
    count = rounded_ref.shape[0]
    whole[...] = total_ref[:, :count] + (
        total_ref[:, count:] + product(low_ref[...], rounded_ref[...], ((1,), (1,)))
    )
    halves(core_ref[0], whole, kept_ref, sent_ref)


def finish_kernel(core_ref, own_ref, other_ref, tfactors_ref, current_ref, high_ref, low_ref, out_ref, joint, packed, out, sems):
    panels, width, _ = tfactors_ref.shape
    count, rows = current_ref.shape
    core = core_ref[0]
    half, rest = joint.shape[0] // 2, packed.shape[0] // 2
    for side, part_ref in ((core, own_ref), (1 - core, other_ref)):
        joint[pl.ds(pl.multiple_of(side * half, 8), half), :] = part_ref[:half, :]
        packed[pl.ds(pl.multiple_of(side * rest, 8), rest), :] = part_ref[half:, :]
    gram = {}
    for i, pair in enumerate(pairs_of(panels)):
        at = i // 2 * width
        gram[pair] = packed[at : at + width, i % 2 * width : (i % 2 + 1) * width]
    exact = functools.partial(product, contract=((1,), (0,)), precision=lax.Precision.HIGHEST)
    scaled = [exact(tfactors_ref[p], joint[p * width : (p + 1) * width, :]) for p in range(panels)]
    links = {(p, q): exact(tfactors_ref[p], gram[p, q]) for p, q in gram}
    for q in range(panels - 1, 0, -1):
        for p in range(q):
            scaled[p] = scaled[p] - exact(links[p, q], scaled[q])
    high, low = split(jnp.concatenate(scaled, axis=0).T)
    both = jnp.concatenate([high, low], axis=0)
    copies = []
    for step in range(rows // OUT_COLUMNS):
        columns = pl.ds(step * OUT_COLUMNS, OUT_COLUMNS)
        first = product(both, high_ref[:, columns], ((1,), (0,)))
        second = product(high, low_ref[:, columns], ((1,), (0,)))
        out[:, columns] = current_ref[:, columns] - (first[:count] + (first[count:] + second))
        copy = pltpu.make_async_copy(out.at[:, columns], out_ref.at[:, columns], sems.at[step])
        copy.start()
        copies.append(copy)
    for copy in copies:
        copy.wait()


def in_vmem(value):
    return pltpu.with_memory_space_constraint(value, pltpu.VMEM)


def in_hbm(value):
    return pltpu.with_memory_space_constraint(value, pltpu.HBM)


def gram_call(core, householder):
    panels, width, rows = householder.shape
    size = panels * width
    height = len(pairs_of(panels)) // 2 * width
    return pl.pallas_call(
        gram_kernel,
        out_shape=(
            pltpu.HBM((size, rows), jnp.bfloat16),
            pltpu.HBM((size, rows), jnp.bfloat16),
            jax.ShapeDtypeStruct((height // 2, 2 * width), jnp.float32),
            jax.ShapeDtypeStruct((height // 2, 2 * width), jnp.float32),
        ),
        grid=(rows // COLUMNS,),
        in_specs=[IN_SMEM, pl.BlockSpec((panels, width, COLUMNS), lambda i: (0, 0, i))],
        out_specs=(
            pl.BlockSpec((size, COLUMNS), lambda i: (0, i)),
            pl.BlockSpec((size, COLUMNS), lambda i: (0, i)),
            pl.BlockSpec((height // 2, 2 * width), lambda i: (0, 0)),
            pl.BlockSpec((height // 2, 2 * width), lambda i: (0, 0)),
        ),
        scratch_shapes=[pltpu.VMEM((size, size), jnp.float32), pltpu.VMEM((height, 2 * width), jnp.float32)],
        compiler_params=pltpu.CompilerParams(vmem_limit_bytes=LIMIT),
        cost_estimate=pl.CostEstimate(flops=10 * 8 * size * size * rows, bytes_accessed=8 * size * rows, transcendentals=0),
        name="gram",
    )(core, in_hbm(householder))


def local_call(kernel, outs, specs, operands, copies=0):
    return pl.pallas_call(
        kernel,
        out_shape=outs,
        in_specs=[IN_SMEM] + specs,
        out_specs=tuple(IN_HBM if out.memory_space == pltpu.HBM else IN_VMEM for out in outs),
        scratch_shapes=[pltpu.SemaphoreType.DMA((copies,))] if copies else [],
        compiler_params=pltpu.CompilerParams(vmem_limit_bytes=LIMIT),
        name=kernel.__name__,
    )(*operands)


def even_call(place, vectors, planes):
    each, length = vectors.shape
    wide = length // planes
    return pl.pallas_call(
        even_kernel,
        out_shape=pltpu.HBM((planes * 2, each, wide // 4), jnp.float32),
        grid_spec=pltpu.PrefetchScalarGridSpec(
            num_scalar_prefetch=1,
            grid=(planes // 2,),
            in_specs=[pl.BlockSpec((each, wide), lambda k, place_ref: (0, 2 * k + place_ref[0] % 2))],
            out_specs=pl.BlockSpec((4, each, wide // 4), lambda k, place_ref: (k, 0, 0)),
        ),
        compiler_params=pltpu.CompilerParams(vmem_limit_bytes=LIMIT),
        name="even",
    )(place, in_hbm(vectors))


def project_call(core, place, even, odd, high, low, gram, more):
    sources, each, rows = even.shape
    count = 2 * sources * each
    size = high.shape[0]
    current, rounded, total = pl.pallas_call(
        project_high_kernel,
        out_shape=(
            pltpu.VMEM((count, rows), jnp.float32),
            pltpu.VMEM((count, rows), jnp.bfloat16),
            pltpu.VMEM((size, 2 * count), jnp.float32),
        ),
        in_specs=[IN_SMEM] + [IN_VMEM] * 6,
        out_specs=(IN_VMEM, IN_VMEM, IN_VMEM),
        compiler_params=pltpu.CompilerParams(vmem_limit_bytes=LIMIT),
        name="project_high",
    )(place, in_vmem(even), *[in_vmem(part) for part in odd], in_vmem(high))
    kept, sent, gram = pl.pallas_call(
        project_low_kernel,
        out_shape=(
            pltpu.VMEM((size // 2, count), jnp.float32),
            pltpu.VMEM((size // 2, count), jnp.float32),
            pltpu.VMEM(gram.shape, jnp.float32),
        ),
        in_specs=[IN_SMEM] + [IN_VMEM] * 5,
        out_specs=(IN_VMEM, IN_VMEM, IN_VMEM),
        scratch_shapes=[pltpu.VMEM((size, count), jnp.float32)],
        compiler_params=pltpu.CompilerParams(vmem_limit_bytes=LIMIT),
        name="project_low",
    )(core, in_vmem(total), in_vmem(rounded), in_vmem(low), in_vmem(gram), in_vmem(more))
    return current, kept, sent, gram


def finish_call(core, own, other, tfactors, current, high, low):
    count, rows = current.shape
    size = high.shape[0]
    return pl.pallas_call(
        finish_kernel,
        out_shape=jax.ShapeDtypeStruct((count, rows), jnp.float32),
        in_specs=[IN_SMEM] + [IN_VMEM] * 6,
        out_specs=IN_ANY,
        scratch_shapes=[
            pltpu.VMEM((size, count), jnp.float32),
            pltpu.VMEM((2 * own.shape[0] - size, count), jnp.float32),
            pltpu.VMEM((count, rows), jnp.float32),
            pltpu.SemaphoreType.DMA((rows // OUT_COLUMNS,)),
        ],
        compiler_params=pltpu.CompilerParams(vmem_limit_bytes=LIMIT),
        name="finish",
    )(core, in_vmem(own), in_vmem(other), tfactors, in_vmem(current), in_vmem(high), in_vmem(low))


def solution(mesh):
    devices, columns = mesh.shape["row"], mesh.shape["col"]
    planes = devices // 4
    row = ("half", "odd", "y", "core")
    parts = Mesh(mesh.devices.reshape(planes // 2, 2, 2, 2, columns), row + ("col",))

    def swap(value, flip):
        return lax.ppermute(value, row, [(i, i ^ flip) for i in range(devices)])

    def shards(vectors_in, householder, tfactors):
        odd, y, core = lax.axis_index("odd"), lax.axis_index("y"), lax.axis_index("core")
        z = lax.axis_index("half") * 2 + odd
        place = jnp.stack([z, y, core]).astype(jnp.int32)
        core = jnp.reshape(core, (1,)).astype(jnp.int32)
        each, length = vectors_in.shape
        wide = length // planes

        def moved(part, shift):
            return lax.ppermute(part, ("half", "odd"), [(i, (i + shift) % planes) for i in range(planes)])

        def spread(up, down, before):
            block = pltpu.VMEM((2, each, wide // 2), jnp.float32)
            kept, sent = local_call(side_kernel, (block, block), [IN_VMEM, IN_VMEM, IN_ANY], (place, up, down, before))
            block = pltpu.VMEM((2, 2, each, wide // 4), jnp.float32)
            kept, sent = local_call(core_kernel, (block, block), [IN_VMEM, IN_VMEM], (place, kept, swap(sent, 2)))
            return kept, swap(sent, 1)

        block = pltpu.VMEM((each, wide), jnp.float32)
        cut = local_call(cut_kernel, (block,) * len(SHIFTS), [IN_HBM], (place, in_hbm(vectors_in)), len(SHIFTS))
        came = [moved(part, shift) for part, shift in zip(cut, SHIFTS)]
        even = even_call(place, vectors_in, planes)
        even = lax.all_to_all(even, ("half", "y", "core"), split_axis=0, concat_axis=0, tiled=True)
        high, low, kept, sent = gram_call(core, householder)
        gram = kept + swap(sent, 1)
        gram = gram + swap(gram, 2)
        scattered = spread(came[0], came[1], kept) + spread(came[2], came[3], gram)
        gram = gram + swap(gram, 4)
        current, value, sent, gram = project_call(core, place, even, scattered, high, low, gram, swap(gram, 24))
        value = value + swap(sent, 1)
        value = value + swap(value, 2)
        first, third = swap(value, 4), swap(value, 12)
        second = swap(jnp.concatenate([value, gram], axis=0), 8)
        half = value.shape[0]
        value = (value + first) + (second[:half] + third)
        gram = gram + second[half:]
        value = value + swap(value, 24)
        own = jnp.concatenate([value, gram], axis=0)
        other = swap(own, 1)
        return finish_call(core, own, other, tfactors, current, high, low)

    in_specs = (P(("col",) + row, None), P(None, None, row), P())
    out_specs = P("col", row)
    return jax.shard_map(shards, mesh=parts, in_specs=in_specs, out_specs=out_specs, check_vma=False)
```

```python
import functools

import jax
import jax.numpy as jnp
from jax import lax
from jax.experimental import pallas as pl
from jax.experimental.pallas import tpu as pltpu
from jax.sharding import Mesh
from jax.sharding import PartitionSpec as P

COLUMNS = 1024
OUT_COLUMNS = 2048
SHIFTS = (1, -1, 3, -3)
LIMIT = 40 * 1024 * 1024
IN_VMEM = pl.BlockSpec(memory_space=pltpu.VMEM)
IN_SMEM = pl.BlockSpec(memory_space=pltpu.SMEM)
IN_ANY = pl.BlockSpec(memory_space=pl.ANY)
IN_HBM = pl.BlockSpec(memory_space=pltpu.HBM)


def product(left, right, contract, precision=None):
    return lax.dot_general(
        left, right, (contract, ((), ())), precision=precision, preferred_element_type=jnp.float32
    )


def split(value):
    high = value.astype(jnp.bfloat16)
    low = (value - high.astype(jnp.float32)).astype(jnp.bfloat16)
    return high, low


def pairs_of(panels):
    return [(p, q) for p in range(panels) for q in range(p + 1, panels)]


def halves(core, whole, own_ref, other_ref):
    half = whole.shape[0] // 2
    own_ref[...] = whole[pl.ds(pl.multiple_of(core * half, 8), half), :]
    other_ref[...] = whole[pl.ds(pl.multiple_of((1 - core) * half, 8), half), :]


def gram_kernel(core_ref, householder_ref, before_ref, high_ref, low_ref, kept_ref, sent_ref, total, packed):
    del before_ref
    panels, width, columns = householder_ref.shape
    size = panels * width
    step = pl.program_id(0)

    @pl.when(step == 0)
    def _():
        total[...] = jnp.zeros_like(total)

    high, low = split(householder_ref[...].reshape(size, columns))
    high_ref[...] = high
    low_ref[...] = low
    both = jnp.concatenate([high, low], axis=0)
    first = product(both, high, ((1,), (1,)))
    second = product(both, low, ((1,), (1,)))
    total[...] += (first[:size] + first[size:]) + (second[:size] + second[size:])

    @pl.when(step == pl.num_programs(0) - 1)
    def _():
        blocks = [
            total[p * width : (p + 1) * width, q * width : (q + 1) * width] for p, q in pairs_of(panels)
        ]
        for i in range(0, len(blocks), 2):
            at = i // 2 * width
            packed[at : at + width, :] = jnp.concatenate(blocks[i : i + 2], axis=1)
        halves(core_ref[0], packed, kept_ref, sent_ref)


def cut_kernel(place_ref, vectors_ref, *refs):
    outs, sems = refs[:-1], refs[-1]
    wide = outs[0].shape[1]
    planes = vectors_ref.shape[1] // wide
    copies = []
    for i, shift in enumerate(SHIFTS):
        plane = (place_ref[0] + shift + planes) % planes
        columns = pl.ds(pl.multiple_of(plane * wide, 128), wide)
        copies.append(pltpu.make_async_copy(vectors_ref.at[:, columns], outs[i], sems.at[i]))
        copies[i].start()
    for copy in copies:
        copy.wait()


def even_kernel(place_ref, block_ref, before_ref, out_ref):
    del place_ref, before_ref
    number, _, wide = out_ref.shape
    for i in range(number):
        out_ref[i] = block_ref[:, i * wide : (i + 1) * wide]


def side_kernel(place_ref, up_ref, down_ref, before_ref, kept_ref, sent_ref):
    del before_ref
    wide = kept_ref.shape[2]
    y = place_ref[1]
    for i, part_ref in enumerate((up_ref, down_ref)):
        kept_ref[i] = part_ref[:, pl.ds(pl.multiple_of(y * wide, 128), wide)]
        sent_ref[i] = part_ref[:, pl.ds(pl.multiple_of((1 - y) * wide, 128), wide)]


def core_kernel(place_ref, own_ref, got_ref, kept_ref, sent_ref):
    wide = kept_ref.shape[3]
    core = place_ref[2]
    for i, part_ref in enumerate((own_ref, got_ref)):
        kept_ref[i] = part_ref[:, :, pl.ds(pl.multiple_of(core * wide, 128), wide)]
        sent_ref[i] = part_ref[:, :, pl.ds(pl.multiple_of((1 - core) * wide, 128), wide)]


def project_high_kernel(place_ref, even_ref, kept_one_ref, got_one_ref, kept_three_ref, got_three_ref, high_ref, current_ref, rounded_ref, total_ref):
    count, rows = current_ref.shape
    planes = count // (4 * even_ref.shape[1])
    z, y, core = place_ref[0], place_ref[1], place_ref[2]
    pair = 2 * even_ref.shape[1]
    total_ref[...] = jnp.zeros_like(total_ref)
    for step in range(rows // COLUMNS):
        columns = pl.ds(step * COLUMNS, COLUMNS)

        def put(plane, side, block):
            at = pl.multiple_of((plane * 2 + side) * pair, 8)
            current_ref[pl.ds(at, pair), columns] = block

        for k in range(planes // 2):
            for side in range(2):
                at = (2 * k + side) * 2
                put(2 * k + z % 2, side, even_ref[at : at + 2, :, columns].reshape(pair, COLUMNS))
        for shift, kept_ref, got_ref in ((1, kept_one_ref, got_one_ref), (3, kept_three_ref, got_three_ref)):
            for other in range(2):
                for i, by in enumerate((shift, -shift)):
                    kept, got = kept_ref[other, i, :, columns], got_ref[other, i, :, columns]
                    block = jnp.concatenate([jnp.where(core == 0, kept, got), jnp.where(core == 0, got, kept)], axis=0)
                    put((z - by + planes) % planes, y ^ other, block)
        high, low = split(current_ref[:, columns])
        rounded_ref[:, columns] = high
        both = jnp.concatenate([high, low], axis=0)
        total_ref[...] += product(high_ref[:, columns], both, ((1,), (1,)))


def after_kernel(held_ref, before_ref, same_ref):
    del held_ref, before_ref, same_ref


def project_low_kernel(core_ref, total_ref, rounded_ref, low_ref, gram_ref, more_ref, kept_ref, sent_ref, sum_ref, whole):
    sum_ref[...] = gram_ref[...] + more_ref[...]
    count = rounded_ref.shape[0]
    whole[...] = total_ref[:, :count] + (
        total_ref[:, count:] + product(low_ref[...], rounded_ref[...], ((1,), (1,)))
    )
    halves(core_ref[0], whole, kept_ref, sent_ref)


def finish_kernel(core_ref, own_ref, other_ref, tfactors_ref, current_ref, high_ref, low_ref, out_ref, joint, packed, out, sems):
    panels, width, _ = tfactors_ref.shape
    count, rows = current_ref.shape
    core = core_ref[0]
    half, rest = joint.shape[0] // 2, packed.shape[0] // 2
    for side, part_ref in ((core, own_ref), (1 - core, other_ref)):
        joint[pl.ds(pl.multiple_of(side * half, 8), half), :] = part_ref[:half, :]
        packed[pl.ds(pl.multiple_of(side * rest, 8), rest), :] = part_ref[half:, :]
    gram = {}
    for i, pair in enumerate(pairs_of(panels)):
        at = i // 2 * width
        gram[pair] = packed[at : at + width, i % 2 * width : (i % 2 + 1) * width]
    exact = functools.partial(product, contract=((1,), (0,)), precision=lax.Precision.HIGHEST)
    scaled = [exact(tfactors_ref[p], joint[p * width : (p + 1) * width, :]) for p in range(panels)]
    links = {(p, q): exact(tfactors_ref[p], gram[p, q]) for p, q in gram}
    for q in range(panels - 1, 0, -1):
        for p in range(q):
            scaled[p] = scaled[p] - exact(links[p, q], scaled[q])
    high, low = split(jnp.concatenate(scaled, axis=0).T)
    both = jnp.concatenate([high, low], axis=0)
    copies = []
    for step in range(rows // OUT_COLUMNS):
        columns = pl.ds(step * OUT_COLUMNS, OUT_COLUMNS)
        first = product(both, high_ref[:, columns], ((1,), (0,)))
        second = product(high, low_ref[:, columns], ((1,), (0,)))
        out[:, columns] = current_ref[:, columns] - (first[:count] + (first[count:] + second))
        copy = pltpu.make_async_copy(out.at[:, columns], out_ref.at[:, columns], sems.at[step])
        copy.start()
        copies.append(copy)
    for copy in copies:
        copy.wait()


def in_vmem(value):
    return pltpu.with_memory_space_constraint(value, pltpu.VMEM)


def in_hbm(value):
    return pltpu.with_memory_space_constraint(value, pltpu.HBM)


def gram_call(core, householder, before):
    panels, width, rows = householder.shape
    size = panels * width
    height = len(pairs_of(panels)) // 2 * width
    return pl.pallas_call(
        gram_kernel,
        out_shape=(
            pltpu.HBM((size, rows), jnp.bfloat16),
            pltpu.HBM((size, rows), jnp.bfloat16),
            jax.ShapeDtypeStruct((height // 2, 2 * width), jnp.float32),
            jax.ShapeDtypeStruct((height // 2, 2 * width), jnp.float32),
        ),
        grid=(rows // COLUMNS,),
        in_specs=[IN_SMEM, pl.BlockSpec((panels, width, COLUMNS), lambda i: (0, 0, i)), IN_ANY],
        out_specs=(
            pl.BlockSpec((size, COLUMNS), lambda i: (0, i)),
            pl.BlockSpec((size, COLUMNS), lambda i: (0, i)),
            pl.BlockSpec((height // 2, 2 * width), lambda i: (0, 0)),
            pl.BlockSpec((height // 2, 2 * width), lambda i: (0, 0)),
        ),
        scratch_shapes=[pltpu.VMEM((size, size), jnp.float32), pltpu.VMEM((height, 2 * width), jnp.float32)],
        compiler_params=pltpu.CompilerParams(vmem_limit_bytes=LIMIT),
        cost_estimate=pl.CostEstimate(flops=10 * 8 * size * size * rows, bytes_accessed=8 * size * rows, transcendentals=0),
        name="gram",
    )(core, in_hbm(householder), before)


def local_call(kernel, outs, specs, operands, copies=0):
    return pl.pallas_call(
        kernel,
        out_shape=outs,
        in_specs=[IN_SMEM] + specs,
        out_specs=tuple(IN_HBM if out.memory_space == pltpu.HBM else IN_VMEM for out in outs),
        scratch_shapes=[pltpu.SemaphoreType.DMA((copies,))] if copies else [],
        compiler_params=pltpu.CompilerParams(vmem_limit_bytes=LIMIT),
        name=kernel.__name__,
    )(*operands)


def even_call(place, vectors, before, planes):
    each, length = vectors.shape
    wide = length // planes
    return pl.pallas_call(
        even_kernel,
        out_shape=pltpu.HBM((planes * 2, each, wide // 4), jnp.float32),
        grid_spec=pltpu.PrefetchScalarGridSpec(
            num_scalar_prefetch=1,
            grid=(planes // 2,),
            in_specs=[pl.BlockSpec((each, wide), lambda k, place_ref: (0, 2 * k + place_ref[0] % 2)), IN_ANY],
            out_specs=pl.BlockSpec((4, each, wide // 4), lambda k, place_ref: (k, 0, 0)),
        ),
        compiler_params=pltpu.CompilerParams(vmem_limit_bytes=LIMIT),
        name="even",
    )(place, in_hbm(vectors), before)


def after(held, before):
    return pl.pallas_call(
        after_kernel,
        out_shape=pltpu.HBM(held.shape, held.dtype),
        in_specs=[IN_HBM, IN_ANY],
        out_specs=IN_HBM,
        input_output_aliases={0: 0},
        compiler_params=pltpu.CompilerParams(vmem_limit_bytes=1024 * 1024),
        name="after",
    )(in_hbm(held), before)


def project_call(core, place, even, odd, high, low, gram, more):
    sources, each, rows = even.shape
    count = 2 * sources * each
    size = high.shape[0]
    current, rounded, total = pl.pallas_call(
        project_high_kernel,
        out_shape=(
            pltpu.VMEM((count, rows), jnp.float32),
            pltpu.VMEM((count, rows), jnp.bfloat16),
            pltpu.VMEM((size, 2 * count), jnp.float32),
        ),
        in_specs=[IN_SMEM] + [IN_VMEM] * 6,
        out_specs=(IN_VMEM, IN_VMEM, IN_VMEM),
        compiler_params=pltpu.CompilerParams(vmem_limit_bytes=LIMIT),
        name="project_high",
    )(place, in_vmem(even), *[in_vmem(part) for part in odd], in_vmem(high))
    kept, sent, gram = pl.pallas_call(
        project_low_kernel,
        out_shape=(
            pltpu.VMEM((size // 2, count), jnp.float32),
            pltpu.VMEM((size // 2, count), jnp.float32),
            pltpu.VMEM(gram.shape, jnp.float32),
        ),
        in_specs=[IN_SMEM] + [IN_VMEM] * 5,
        out_specs=(IN_VMEM, IN_VMEM, IN_VMEM),
        scratch_shapes=[pltpu.VMEM((size, count), jnp.float32)],
        compiler_params=pltpu.CompilerParams(vmem_limit_bytes=LIMIT),
        name="project_low",
    )(core, in_vmem(total), in_vmem(rounded), in_vmem(low), in_vmem(gram), in_vmem(more))
    return current, kept, sent, gram


def finish_call(core, own, other, tfactors, current, high, low):
    count, rows = current.shape
    size = high.shape[0]
    return pl.pallas_call(
        finish_kernel,
        out_shape=jax.ShapeDtypeStruct((count, rows), jnp.float32),
        in_specs=[IN_SMEM] + [IN_VMEM] * 6,
        out_specs=IN_ANY,
        scratch_shapes=[
            pltpu.VMEM((size, count), jnp.float32),
            pltpu.VMEM((2 * own.shape[0] - size, count), jnp.float32),
            pltpu.VMEM((count, rows), jnp.float32),
            pltpu.SemaphoreType.DMA((rows // OUT_COLUMNS,)),
        ],
        compiler_params=pltpu.CompilerParams(vmem_limit_bytes=LIMIT),
        name="finish",
    )(core, in_vmem(own), in_vmem(other), tfactors, in_vmem(current), in_vmem(high), in_vmem(low))


def solution(mesh):
    devices, columns = mesh.shape["row"], mesh.shape["col"]
    planes = devices // 4
    row = ("half", "odd", "y", "core")
    parts = Mesh(mesh.devices.reshape(planes // 2, 2, 2, 2, columns), row + ("col",))

    def swap(value, flip):
        return lax.ppermute(value, row, [(i, i ^ flip) for i in range(devices)])

    def shards(vectors_in, householder, tfactors):
        odd, y, core = lax.axis_index("odd"), lax.axis_index("y"), lax.axis_index("core")
        z = lax.axis_index("half") * 2 + odd
        place = jnp.stack([z, y, core]).astype(jnp.int32)
        core = jnp.reshape(core, (1,)).astype(jnp.int32)
        each, length = vectors_in.shape
        wide = length // planes

        def moved(part, shift):
            return lax.ppermute(part, ("half", "odd"), [(i, (i + shift) % planes) for i in range(planes)])

        def spread(up, down, before):
            block = pltpu.VMEM((2, each, wide // 2), jnp.float32)
            kept, sent = local_call(side_kernel, (block, block), [IN_VMEM, IN_VMEM, IN_ANY], (place, up, down, before))
            block = pltpu.VMEM((2, 2, each, wide // 4), jnp.float32)
            kept, sent = local_call(core_kernel, (block, block), [IN_VMEM, IN_VMEM], (place, kept, swap(sent, 2)))
            return kept, swap(sent, 1)

        block = pltpu.VMEM((each, wide), jnp.float32)
        cut = local_call(cut_kernel, (block,) * len(SHIFTS), [IN_HBM], (place, in_hbm(vectors_in)), len(SHIFTS))
        came = [moved(part, shift) for part, shift in zip(cut, SHIFTS)]
        even = even_call(place, vectors_in, came[0], planes)
        even = lax.all_to_all(even, ("half", "y", "core"), split_axis=0, concat_axis=0, tiled=True)
        high, low, kept, sent = gram_call(core, householder, came[0])
        gram = kept + swap(sent, 1)
        gram = gram + swap(gram, 2)
        scattered = spread(came[0], came[1], came[0]) + spread(came[2], came[3], gram)
        high = after(high, even)
        current, value, sent, gram = project_call(core, place, even, scattered, high, low, gram, swap(gram, 4))
        value = value + swap(sent, 1)
        value = value + swap(value, 2)
        half = value.shape[0]
        first, third = swap(value, 4), swap(value, 12)
        second = swap(jnp.concatenate([value, gram], axis=0), 8)
        own = jnp.concatenate([(value + first) + (second[:half] + third), gram + second[half:]], axis=0)
        own = own + swap(own, 24)
        other = swap(own, 1)
        return finish_call(core, own, other, tfactors, current, high, low)

    in_specs = (P(("col",) + row, None), P(None, None, row), P())
    out_specs = P("col", row)
    return jax.shard_map(shards, mesh=parts, in_specs=in_specs, out_specs=out_specs, check_vma=False)
```

```python
import functools

import jax
import jax.numpy as jnp
from jax import lax
from jax.experimental import pallas as pl
from jax.experimental.pallas import tpu as pltpu
from jax.sharding import Mesh
from jax.sharding import PartitionSpec as P

COLUMNS = 1024
OUT_COLUMNS = 2048
SHIFTS = (1, -1, 3, -3)
LIMIT = 40 * 1024 * 1024
IN_VMEM = pl.BlockSpec(memory_space=pltpu.VMEM)
IN_SMEM = pl.BlockSpec(memory_space=pltpu.SMEM)
IN_ANY = pl.BlockSpec(memory_space=pl.ANY)
IN_HBM = pl.BlockSpec(memory_space=pltpu.HBM)


def product(left, right, contract, precision=None):
    return lax.dot_general(
        left, right, (contract, ((), ())), precision=precision, preferred_element_type=jnp.float32
    )


def split(value):
    high = value.astype(jnp.bfloat16)
    low = (value - high.astype(jnp.float32)).astype(jnp.bfloat16)
    return high, low


def pairs_of(panels):
    return [(p, q) for p in range(panels) for q in range(p + 1, panels)]


def halves(core, whole, own_ref, other_ref):
    half = whole.shape[0] // 2
    own_ref[...] = whole[pl.ds(pl.multiple_of(core * half, 8), half), :]
    other_ref[...] = whole[pl.ds(pl.multiple_of((1 - core) * half, 8), half), :]


def gram_kernel(core_ref, householder_ref, before_ref, high_ref, low_ref, kept_ref, sent_ref, total, packed):
    del before_ref
    panels, width, columns = householder_ref.shape
    size = panels * width
    step = pl.program_id(0)

    @pl.when(step == 0)
    def _():
        total[...] = jnp.zeros_like(total)

    high, low = split(householder_ref[...].reshape(size, columns))
    high_ref[...] = high
    low_ref[...] = low
    both = jnp.concatenate([high, low], axis=0)
    first = product(both, high, ((1,), (1,)))
    second = product(both, low, ((1,), (1,)))
    total[...] += (first[:size] + first[size:]) + (second[:size] + second[size:])

    @pl.when(step == pl.num_programs(0) - 1)
    def _():
        blocks = [
            total[p * width : (p + 1) * width, q * width : (q + 1) * width] for p, q in pairs_of(panels)
        ]
        for i in range(0, len(blocks), 2):
            at = i // 2 * width
            packed[at : at + width, :] = jnp.concatenate(blocks[i : i + 2], axis=1)
        halves(core_ref[0], packed, kept_ref, sent_ref)


def cut_kernel(place_ref, vectors_ref, *refs):
    outs, sems = refs[:-1], refs[-1]
    wide = outs[0].shape[1]
    planes = vectors_ref.shape[1] // wide
    copies = []
    for i, shift in enumerate(SHIFTS):
        plane = (place_ref[0] + shift + planes) % planes
        columns = pl.ds(pl.multiple_of(plane * wide, 128), wide)
        copies.append(pltpu.make_async_copy(vectors_ref.at[:, columns], outs[i], sems.at[i]))
        copies[i].start()
    for copy in copies:
        copy.wait()


def even_kernel(place_ref, block_ref, before_ref, out_ref):
    del place_ref, before_ref
    number, _, wide = out_ref.shape
    for i in range(number):
        out_ref[i] = block_ref[:, i * wide : (i + 1) * wide]


def side_kernel(place_ref, up_ref, down_ref, before_ref, kept_ref, sent_ref):
    del before_ref
    wide = kept_ref.shape[2]
    y = place_ref[1]
    for i, part_ref in enumerate((up_ref, down_ref)):
        kept_ref[i] = part_ref[:, pl.ds(pl.multiple_of(y * wide, 128), wide)]
        sent_ref[i] = part_ref[:, pl.ds(pl.multiple_of((1 - y) * wide, 128), wide)]


def core_kernel(place_ref, own_ref, got_ref, kept_ref, sent_ref):
    wide = kept_ref.shape[3]
    core = place_ref[2]
    for i, part_ref in enumerate((own_ref, got_ref)):
        kept_ref[i] = part_ref[:, :, pl.ds(pl.multiple_of(core * wide, 128), wide)]
        sent_ref[i] = part_ref[:, :, pl.ds(pl.multiple_of((1 - core) * wide, 128), wide)]


def project_high_kernel(place_ref, even_ref, kept_one_ref, got_one_ref, kept_three_ref, got_three_ref, high_ref, current_ref, rounded_ref, total_ref):
    count, rows = current_ref.shape
    planes = count // (4 * even_ref.shape[1])
    z, y, core = place_ref[0], place_ref[1], place_ref[2]
    pair = 2 * even_ref.shape[1]
    total_ref[...] = jnp.zeros_like(total_ref)
    for step in range(rows // COLUMNS):
        columns = pl.ds(step * COLUMNS, COLUMNS)

        def put(plane, side, block):
            at = pl.multiple_of((plane * 2 + side) * pair, 8)
            current_ref[pl.ds(at, pair), columns] = block

        for k in range(planes // 2):
            for side in range(2):
                at = (2 * k + side) * 2
                put(2 * k + z % 2, side, even_ref[at : at + 2, :, columns].reshape(pair, COLUMNS))
        for shift, kept_ref, got_ref in ((1, kept_one_ref, got_one_ref), (3, kept_three_ref, got_three_ref)):
            for other in range(2):
                for i, by in enumerate((shift, -shift)):
                    kept, got = kept_ref[other, i, :, columns], got_ref[other, i, :, columns]
                    block = jnp.concatenate([jnp.where(core == 0, kept, got), jnp.where(core == 0, got, kept)], axis=0)
                    put((z - by + planes) % planes, y ^ other, block)
        high, low = split(current_ref[:, columns])
        rounded_ref[:, columns] = high
        both = jnp.concatenate([high, low], axis=0)
        total_ref[...] += product(high_ref[:, columns], both, ((1,), (1,)))


def after_kernel(held_ref, before_ref, same_ref):
    del held_ref, before_ref, same_ref


def project_low_kernel(core_ref, total_ref, rounded_ref, low_ref, gram_ref, more_ref, kept_ref, sent_ref, sum_ref, whole):
    sum_ref[...] = gram_ref[...] + more_ref[...]
    count = rounded_ref.shape[0]
    whole[...] = total_ref[:, :count] + (
        total_ref[:, count:] + product(low_ref[...], rounded_ref[...], ((1,), (1,)))
    )
    halves(core_ref[0], whole, kept_ref, sent_ref)


def finish_kernel(core_ref, own_ref, other_ref, tfactors_ref, current_ref, high_ref, low_ref, out_ref, joint, packed, out, sems):
    panels, width, _ = tfactors_ref.shape
    count, rows = current_ref.shape
    core = core_ref[0]
    half, rest = joint.shape[0] // 2, packed.shape[0] // 2
    for side, part_ref in ((core, own_ref), (1 - core, other_ref)):
        joint[pl.ds(pl.multiple_of(side * half, 8), half), :] = part_ref[:half, :]
        packed[pl.ds(pl.multiple_of(side * rest, 8), rest), :] = part_ref[half:, :]
    gram = {}
    for i, pair in enumerate(pairs_of(panels)):
        at = i // 2 * width
        gram[pair] = packed[at : at + width, i % 2 * width : (i % 2 + 1) * width]
    exact = functools.partial(product, contract=((1,), (0,)), precision=lax.Precision.HIGHEST)
    scaled = [exact(tfactors_ref[p], joint[p * width : (p + 1) * width, :]) for p in range(panels)]
    links = {(p, q): exact(tfactors_ref[p], gram[p, q]) for p, q in gram}
    for q in range(panels - 1, 0, -1):
        for p in range(q):
            scaled[p] = scaled[p] - exact(links[p, q], scaled[q])
    high, low = split(jnp.concatenate(scaled, axis=0).T)
    both = jnp.concatenate([high, low], axis=0)
    copies = []
    for step in range(rows // OUT_COLUMNS):
        columns = pl.ds(step * OUT_COLUMNS, OUT_COLUMNS)
        first = product(both, high_ref[:, columns], ((1,), (0,)))
        second = product(high, low_ref[:, columns], ((1,), (0,)))
        out[:, columns] = current_ref[:, columns] - (first[:count] + (first[count:] + second))
        copy = pltpu.make_async_copy(out.at[:, columns], out_ref.at[:, columns], sems.at[step])
        copy.start()
        copies.append(copy)
    for copy in copies:
        copy.wait()


def in_vmem(value):
    return pltpu.with_memory_space_constraint(value, pltpu.VMEM)


def in_hbm(value):
    return pltpu.with_memory_space_constraint(value, pltpu.HBM)


def gram_call(core, householder, before):
    panels, width, rows = householder.shape
    size = panels * width
    height = len(pairs_of(panels)) // 2 * width
    return pl.pallas_call(
        gram_kernel,
        out_shape=(
            pltpu.HBM((size, rows), jnp.bfloat16),
            pltpu.HBM((size, rows), jnp.bfloat16),
            jax.ShapeDtypeStruct((height // 2, 2 * width), jnp.float32),
            jax.ShapeDtypeStruct((height // 2, 2 * width), jnp.float32),
        ),
        grid=(rows // COLUMNS,),
        in_specs=[IN_SMEM, pl.BlockSpec((panels, width, COLUMNS), lambda i: (0, 0, i)), IN_ANY],
        out_specs=(
            pl.BlockSpec((size, COLUMNS), lambda i: (0, i)),
            pl.BlockSpec((size, COLUMNS), lambda i: (0, i)),
            pl.BlockSpec((height // 2, 2 * width), lambda i: (0, 0)),
            pl.BlockSpec((height // 2, 2 * width), lambda i: (0, 0)),
        ),
        scratch_shapes=[pltpu.VMEM((size, size), jnp.float32), pltpu.VMEM((height, 2 * width), jnp.float32)],
        compiler_params=pltpu.CompilerParams(vmem_limit_bytes=LIMIT),
        cost_estimate=pl.CostEstimate(flops=10 * 8 * size * size * rows, bytes_accessed=8 * size * rows, transcendentals=0),
        name="gram",
    )(core, in_hbm(householder), before)


def local_call(kernel, outs, specs, operands, copies=0):
    return pl.pallas_call(
        kernel,
        out_shape=outs,
        in_specs=[IN_SMEM] + specs,
        out_specs=tuple(IN_HBM if out.memory_space == pltpu.HBM else IN_VMEM for out in outs),
        scratch_shapes=[pltpu.SemaphoreType.DMA((copies,))] if copies else [],
        compiler_params=pltpu.CompilerParams(vmem_limit_bytes=LIMIT),
        name=kernel.__name__,
    )(*operands)


def even_call(place, vectors, before, planes):
    each, length = vectors.shape
    wide = length // planes
    return pl.pallas_call(
        even_kernel,
        out_shape=pltpu.HBM((planes * 2, each, wide // 4), jnp.float32),
        grid_spec=pltpu.PrefetchScalarGridSpec(
            num_scalar_prefetch=1,
            grid=(planes // 2,),
            in_specs=[pl.BlockSpec((each, wide), lambda k, place_ref: (0, 2 * k + place_ref[0] % 2)), IN_ANY],
            out_specs=pl.BlockSpec((4, each, wide // 4), lambda k, place_ref: (k, 0, 0)),
        ),
        compiler_params=pltpu.CompilerParams(vmem_limit_bytes=LIMIT),
        name="even",
    )(place, in_hbm(vectors), before)


def after(held, before):
    return pl.pallas_call(
        after_kernel,
        out_shape=pltpu.HBM(held.shape, held.dtype),
        in_specs=[IN_HBM, IN_ANY],
        out_specs=IN_HBM,
        input_output_aliases={0: 0},
        compiler_params=pltpu.CompilerParams(vmem_limit_bytes=1024 * 1024),
        name="after",
    )(in_hbm(held), before)


def project_call(core, place, even, odd, high, low, gram, more):
    sources, each, rows = even.shape
    count = 2 * sources * each
    size = high.shape[0]
    current, rounded, total = pl.pallas_call(
        project_high_kernel,
        out_shape=(
            pltpu.VMEM((count, rows), jnp.float32),
            pltpu.VMEM((count, rows), jnp.bfloat16),
            pltpu.VMEM((size, 2 * count), jnp.float32),
        ),
        in_specs=[IN_SMEM] + [IN_VMEM] * 6,
        out_specs=(IN_VMEM, IN_VMEM, IN_VMEM),
        compiler_params=pltpu.CompilerParams(vmem_limit_bytes=LIMIT),
        name="project_high",
    )(place, in_vmem(even), *[in_vmem(part) for part in odd], in_vmem(high))
    kept, sent, gram = pl.pallas_call(
        project_low_kernel,
        out_shape=(
            pltpu.VMEM((size // 2, count), jnp.float32),
            pltpu.VMEM((size // 2, count), jnp.float32),
            pltpu.VMEM(gram.shape, jnp.float32),
        ),
        in_specs=[IN_SMEM] + [IN_VMEM] * 5,
        out_specs=(IN_VMEM, IN_VMEM, IN_VMEM),
        scratch_shapes=[pltpu.VMEM((size, count), jnp.float32)],
        compiler_params=pltpu.CompilerParams(vmem_limit_bytes=LIMIT),
        name="project_low",
    )(core, in_vmem(total), in_vmem(rounded), in_vmem(low), in_vmem(gram), in_vmem(more))
    return current, kept, sent, gram


def finish_call(core, own, other, tfactors, current, high, low):
    count, rows = current.shape
    size = high.shape[0]
    return pl.pallas_call(
        finish_kernel,
        out_shape=jax.ShapeDtypeStruct((count, rows), jnp.float32),
        in_specs=[IN_SMEM] + [IN_VMEM] * 6,
        out_specs=IN_ANY,
        scratch_shapes=[
            pltpu.VMEM((size, count), jnp.float32),
            pltpu.VMEM((2 * own.shape[0] - size, count), jnp.float32),
            pltpu.VMEM((count, rows), jnp.float32),
            pltpu.SemaphoreType.DMA((rows // OUT_COLUMNS,)),
        ],
        compiler_params=pltpu.CompilerParams(vmem_limit_bytes=LIMIT),
        name="finish",
    )(core, in_vmem(own), in_vmem(other), tfactors, in_vmem(current), in_vmem(high), in_vmem(low))


def solution(mesh):
    devices, columns = mesh.shape["row"], mesh.shape["col"]
    planes = devices // 4
    row = ("half", "odd", "y", "core")
    parts = Mesh(mesh.devices.reshape(planes // 2, 2, 2, 2, columns), row + ("col",))

    def swap(value, flip):
        return lax.ppermute(value, row, [(i, i ^ flip) for i in range(devices)])

    def shards(vectors_in, householder, tfactors):
        odd, y, core = lax.axis_index("odd"), lax.axis_index("y"), lax.axis_index("core")
        z = lax.axis_index("half") * 2 + odd
        place = jnp.stack([z, y, core]).astype(jnp.int32)
        core = jnp.reshape(core, (1,)).astype(jnp.int32)
        each, length = vectors_in.shape
        wide = length // planes

        def moved(part, shift):
            return lax.ppermute(part, ("half", "odd"), [(i, (i + shift) % planes) for i in range(planes)])

        def sides(up, down, before):
            block = pltpu.VMEM((2, each, wide // 2), jnp.float32)
            return local_call(side_kernel, (block, block), [IN_VMEM, IN_VMEM, IN_ANY], (place, up, down, before))

        def spread(kept, got):
            block = pltpu.VMEM((2, 2, each, wide // 4), jnp.float32)
            kept, sent = local_call(core_kernel, (block, block), [IN_VMEM, IN_VMEM], (place, kept, got))
            return kept, swap(sent, 1)

        block = pltpu.VMEM((each, wide), jnp.float32)
        cut = local_call(cut_kernel, (block,) * len(SHIFTS), [IN_HBM], (place, in_hbm(vectors_in)), len(SHIFTS))
        came = [moved(part, shift) for part, shift in zip(cut, SHIFTS)]
        packed = even_call(place, vectors_in, came[0], planes)
        even = lax.all_to_all(packed, ("half", "y", "core"), split_axis=0, concat_axis=0, tiled=True)
        one_kept, one_sent = sides(came[0], came[1], came[0])
        one_got = swap(one_sent, 2)
        high, low, kept, sent = gram_call(core, householder, came[0])
        gram = kept + swap(sent, 1)
        gram = gram + swap(gram, 2)
        three_kept, three_sent = sides(came[2], came[3], kept)
        three_got = swap(three_sent, 2)
        scattered = spread(one_kept, one_got) + spread(three_kept, three_got)
        high = after(high, even)
        current, value, sent, gram = project_call(core, place, even, scattered, high, low, gram, swap(gram, 4))
        value = value + swap(sent, 1)
        value = value + swap(value, 2)
        half = value.shape[0]
        first, third = swap(value, 4), swap(value, 12)
        second = swap(jnp.concatenate([value, gram], axis=0), 8)
        own = jnp.concatenate([(value + first) + (second[:half] + third), gram + second[half:]], axis=0)
        own = own + swap(own, 24)
        other = swap(own, 1)
        return finish_call(core, own, other, tfactors, current, high, low)

    in_specs = (P(("col",) + row, None), P(None, None, row), P())
    out_specs = P("col", row)
    return jax.shard_map(shards, mesh=parts, in_specs=in_specs, out_specs=out_specs, check_vma=False)
```

```python
import functools

import jax
import jax.numpy as jnp
from jax import lax
from jax.experimental import pallas as pl
from jax.experimental.pallas import tpu as pltpu
from jax.sharding import Mesh
from jax.sharding import PartitionSpec as P

COLUMNS = 1024
OUT_COLUMNS = 2048
SHIFTS = (1, -1, 3, -3)
LIMIT = 40 * 1024 * 1024
IN_VMEM = pl.BlockSpec(memory_space=pltpu.VMEM)
IN_SMEM = pl.BlockSpec(memory_space=pltpu.SMEM)
IN_ANY = pl.BlockSpec(memory_space=pl.ANY)
IN_HBM = pl.BlockSpec(memory_space=pltpu.HBM)


def product(left, right, contract, precision=None):
    return lax.dot_general(
        left, right, (contract, ((), ())), precision=precision, preferred_element_type=jnp.float32
    )


def split(value):
    high = value.astype(jnp.bfloat16)
    low = (value - high.astype(jnp.float32)).astype(jnp.bfloat16)
    return high, low


def pairs_of(panels):
    return [(p, q) for p in range(panels) for q in range(p + 1, panels)]


def halves(core, whole, own_ref, other_ref):
    half = whole.shape[0] // 2
    own_ref[...] = whole[pl.ds(pl.multiple_of(core * half, 8), half), :]
    other_ref[...] = whole[pl.ds(pl.multiple_of((1 - core) * half, 8), half), :]


def gram_kernel(core_ref, householder_ref, before_ref, high_ref, low_ref, kept_ref, sent_ref, total, packed):
    del before_ref
    panels, width, columns = householder_ref.shape
    size = panels * width
    step = pl.program_id(0)

    @pl.when(step == 0)
    def _():
        total[...] = jnp.zeros_like(total)

    high, low = split(householder_ref[...].reshape(size, columns))
    high_ref[...] = high
    low_ref[...] = low
    both = jnp.concatenate([high, low], axis=0)
    first = product(both, high, ((1,), (1,)))
    second = product(both, low, ((1,), (1,)))
    total[...] += (first[:size] + first[size:]) + (second[:size] + second[size:])

    @pl.when(step == pl.num_programs(0) - 1)
    def _():
        blocks = [
            total[p * width : (p + 1) * width, q * width : (q + 1) * width] for p, q in pairs_of(panels)
        ]
        for i in range(0, len(blocks), 2):
            at = i // 2 * width
            packed[at : at + width, :] = jnp.concatenate(blocks[i : i + 2], axis=1)
        halves(core_ref[0], packed, kept_ref, sent_ref)


def cut_kernel(place_ref, vectors_ref, *refs):
    outs, sems = refs[:-1], refs[-1]
    wide = outs[0].shape[1]
    planes = vectors_ref.shape[1] // wide
    copies = []
    for i, shift in enumerate(SHIFTS):
        plane = (place_ref[0] + shift + planes) % planes
        columns = pl.ds(pl.multiple_of(plane * wide, 128), wide)
        copies.append(pltpu.make_async_copy(vectors_ref.at[:, columns], outs[i], sems.at[i]))
        copies[i].start()
    for copy in copies:
        copy.wait()


def even_kernel(place_ref, block_ref, before_ref, out_ref):
    del place_ref, before_ref
    number, _, wide = out_ref.shape
    for i in range(number):
        out_ref[i] = block_ref[:, i * wide : (i + 1) * wide]


def side_kernel(place_ref, up_ref, down_ref, before_ref, kept_ref, sent_ref):
    del before_ref
    wide = kept_ref.shape[2]
    y = place_ref[1]
    for i, part_ref in enumerate((up_ref, down_ref)):
        kept_ref[i] = part_ref[:, pl.ds(pl.multiple_of(y * wide, 128), wide)]
        sent_ref[i] = part_ref[:, pl.ds(pl.multiple_of((1 - y) * wide, 128), wide)]


def core_kernel(place_ref, own_ref, got_ref, kept_ref, sent_ref):
    wide = kept_ref.shape[3]
    core = place_ref[2]
    for i, part_ref in enumerate((own_ref, got_ref)):
        kept_ref[i] = part_ref[:, :, pl.ds(pl.multiple_of(core * wide, 128), wide)]
        sent_ref[i] = part_ref[:, :, pl.ds(pl.multiple_of((1 - core) * wide, 128), wide)]


def project_high_kernel(place_ref, even_ref, kept_one_ref, got_one_ref, kept_three_ref, got_three_ref, high_ref, current_ref, rounded_ref, total_ref):
    count, rows = current_ref.shape
    planes = count // (4 * even_ref.shape[1])
    z, y, core = place_ref[0], place_ref[1], place_ref[2]
    pair = 2 * even_ref.shape[1]
    total_ref[...] = jnp.zeros_like(total_ref)
    for step in range(rows // COLUMNS):
        columns = pl.ds(step * COLUMNS, COLUMNS)

        def put(plane, side, block):
            at = pl.multiple_of((plane * 2 + side) * pair, 8)
            current_ref[pl.ds(at, pair), columns] = block

        for k in range(planes // 2):
            for side in range(2):
                at = (2 * k + side) * 2
                put(2 * k + z % 2, side, even_ref[at : at + 2, :, columns].reshape(pair, COLUMNS))
        for shift, kept_ref, got_ref in ((1, kept_one_ref, got_one_ref), (3, kept_three_ref, got_three_ref)):
            for other in range(2):
                for i, by in enumerate((shift, -shift)):
                    kept, got = kept_ref[other, i, :, columns], got_ref[other, i, :, columns]
                    block = jnp.concatenate([jnp.where(core == 0, kept, got), jnp.where(core == 0, got, kept)], axis=0)
                    put((z - by + planes) % planes, y ^ other, block)
        high, low = split(current_ref[:, columns])
        rounded_ref[:, columns] = high
        both = jnp.concatenate([high, low], axis=0)
        total_ref[...] += product(high_ref[:, columns], both, ((1,), (1,)))


def after_kernel(held_ref, before_ref, same_ref):
    del held_ref, before_ref, same_ref


def project_low_kernel(core_ref, total_ref, rounded_ref, low_ref, gram_ref, more_ref, kept_ref, sent_ref, sum_ref, whole):
    sum_ref[...] = gram_ref[...] + more_ref[...]
    count = rounded_ref.shape[0]
    whole[...] = total_ref[:, :count] + (
        total_ref[:, count:] + product(low_ref[...], rounded_ref[...], ((1,), (1,)))
    )
    halves(core_ref[0], whole, kept_ref, sent_ref)


def finish_kernel(core_ref, own_ref, other_ref, tfactors_ref, current_ref, high_ref, low_ref, out_ref, joint, packed, out, sems):
    panels, width, _ = tfactors_ref.shape
    count, rows = current_ref.shape
    core = core_ref[0]
    half, rest = joint.shape[0] // 2, packed.shape[0] // 2
    for side, part_ref in ((core, own_ref), (1 - core, other_ref)):
        joint[pl.ds(pl.multiple_of(side * half, 8), half), :] = part_ref[:half, :]
        packed[pl.ds(pl.multiple_of(side * rest, 8), rest), :] = part_ref[half:, :]
    gram = {}
    for i, pair in enumerate(pairs_of(panels)):
        at = i // 2 * width
        gram[pair] = packed[at : at + width, i % 2 * width : (i % 2 + 1) * width]
    exact = functools.partial(product, contract=((1,), (0,)), precision=lax.Precision.HIGHEST)
    scaled = [exact(tfactors_ref[p], joint[p * width : (p + 1) * width, :]) for p in range(panels)]
    links = {(p, q): exact(tfactors_ref[p], gram[p, q]) for p, q in gram}
    for q in range(panels - 1, 0, -1):
        for p in range(q):
            scaled[p] = scaled[p] - exact(links[p, q], scaled[q])
    high, low = split(jnp.concatenate(scaled, axis=0).T)
    both = jnp.concatenate([high, low], axis=0)
    copies = []
    for step in range(rows // OUT_COLUMNS):
        columns = pl.ds(step * OUT_COLUMNS, OUT_COLUMNS)
        first = product(both, high_ref[:, columns], ((1,), (0,)))
        second = product(high, low_ref[:, columns], ((1,), (0,)))
        out[:, columns] = current_ref[:, columns] - (first[:count] + (first[count:] + second))
        copy = pltpu.make_async_copy(out.at[:, columns], out_ref.at[:, columns], sems.at[step])
        copy.start()
        copies.append(copy)
    for copy in copies:
        copy.wait()


def in_vmem(value):
    return pltpu.with_memory_space_constraint(value, pltpu.VMEM)


def in_hbm(value):
    return pltpu.with_memory_space_constraint(value, pltpu.HBM)


def gram_call(core, householder, before):
    panels, width, rows = householder.shape
    size = panels * width
    height = len(pairs_of(panels)) // 2 * width
    return pl.pallas_call(
        gram_kernel,
        out_shape=(
            pltpu.HBM((size, rows), jnp.bfloat16),
            pltpu.HBM((size, rows), jnp.bfloat16),
            jax.ShapeDtypeStruct((height // 2, 2 * width), jnp.float32),
            jax.ShapeDtypeStruct((height // 2, 2 * width), jnp.float32),
        ),
        grid=(rows // COLUMNS,),
        in_specs=[IN_SMEM, pl.BlockSpec((panels, width, COLUMNS), lambda i: (0, 0, i)), IN_ANY],
        out_specs=(
            pl.BlockSpec((size, COLUMNS), lambda i: (0, i)),
            pl.BlockSpec((size, COLUMNS), lambda i: (0, i)),
            pl.BlockSpec((height // 2, 2 * width), lambda i: (0, 0)),
            pl.BlockSpec((height // 2, 2 * width), lambda i: (0, 0)),
        ),
        scratch_shapes=[pltpu.VMEM((size, size), jnp.float32), pltpu.VMEM((height, 2 * width), jnp.float32)],
        compiler_params=pltpu.CompilerParams(vmem_limit_bytes=LIMIT),
        cost_estimate=pl.CostEstimate(flops=10 * 8 * size * size * rows, bytes_accessed=8 * size * rows, transcendentals=0),
        name="gram",
    )(core, in_hbm(householder), before)


def local_call(kernel, outs, specs, operands, copies=0):
    return pl.pallas_call(
        kernel,
        out_shape=outs,
        in_specs=[IN_SMEM] + specs,
        out_specs=tuple(IN_HBM if out.memory_space == pltpu.HBM else IN_VMEM for out in outs),
        scratch_shapes=[pltpu.SemaphoreType.DMA((copies,))] if copies else [],
        compiler_params=pltpu.CompilerParams(vmem_limit_bytes=LIMIT),
        name=kernel.__name__,
    )(*operands)


def even_call(place, vectors, before, planes):
    each, length = vectors.shape
    wide = length // planes
    return pl.pallas_call(
        even_kernel,
        out_shape=pltpu.HBM((planes * 2, each, wide // 4), jnp.float32),
        grid_spec=pltpu.PrefetchScalarGridSpec(
            num_scalar_prefetch=1,
            grid=(planes // 2,),
            in_specs=[pl.BlockSpec((each, wide), lambda k, place_ref: (0, 2 * k + place_ref[0] % 2)), IN_ANY],
            out_specs=pl.BlockSpec((4, each, wide // 4), lambda k, place_ref: (k, 0, 0)),
        ),
        compiler_params=pltpu.CompilerParams(vmem_limit_bytes=LIMIT),
        name="even",
    )(place, in_hbm(vectors), before)


def after(held, before):
    return pl.pallas_call(
        after_kernel,
        out_shape=pltpu.HBM(held.shape, held.dtype),
        in_specs=[IN_HBM, IN_ANY],
        out_specs=IN_HBM,
        input_output_aliases={0: 0},
        compiler_params=pltpu.CompilerParams(vmem_limit_bytes=1024 * 1024),
        name="after",
    )(in_hbm(held), before)


def project_call(core, place, even, odd, high, low, gram, more):
    sources, each, rows = even.shape
    count = 2 * sources * each
    size = high.shape[0]
    current, rounded, total = pl.pallas_call(
        project_high_kernel,
        out_shape=(
            pltpu.VMEM((count, rows), jnp.float32),
            pltpu.VMEM((count, rows), jnp.bfloat16),
            pltpu.VMEM((size, 2 * count), jnp.float32),
        ),
        in_specs=[IN_SMEM] + [IN_VMEM] * 6,
        out_specs=(IN_VMEM, IN_VMEM, IN_VMEM),
        compiler_params=pltpu.CompilerParams(vmem_limit_bytes=LIMIT),
        name="project_high",
    )(place, in_vmem(even), *[in_vmem(part) for part in odd], in_vmem(high))
    kept, sent, gram = pl.pallas_call(
        project_low_kernel,
        out_shape=(
            pltpu.VMEM((size // 2, count), jnp.float32),
            pltpu.VMEM((size // 2, count), jnp.float32),
            pltpu.VMEM(gram.shape, jnp.float32),
        ),
        in_specs=[IN_SMEM] + [IN_VMEM] * 5,
        out_specs=(IN_VMEM, IN_VMEM, IN_VMEM),
        scratch_shapes=[pltpu.VMEM((size, count), jnp.float32)],
        compiler_params=pltpu.CompilerParams(vmem_limit_bytes=LIMIT),
        name="project_low",
    )(core, in_vmem(total), in_vmem(rounded), in_vmem(low), in_vmem(gram), in_vmem(more))
    return current, kept, sent, gram


def finish_call(core, own, other, tfactors, current, high, low):
    count, rows = current.shape
    size = high.shape[0]
    return pl.pallas_call(
        finish_kernel,
        out_shape=jax.ShapeDtypeStruct((count, rows), jnp.float32),
        in_specs=[IN_SMEM] + [IN_VMEM] * 6,
        out_specs=IN_ANY,
        scratch_shapes=[
            pltpu.VMEM((size, count), jnp.float32),
            pltpu.VMEM((2 * own.shape[0] - size, count), jnp.float32),
            pltpu.VMEM((count, rows), jnp.float32),
            pltpu.SemaphoreType.DMA((rows // OUT_COLUMNS,)),
        ],
        compiler_params=pltpu.CompilerParams(vmem_limit_bytes=LIMIT),
        name="finish",
    )(core, in_vmem(own), in_vmem(other), tfactors, in_vmem(current), in_vmem(high), in_vmem(low))


def solution(mesh):
    devices, columns = mesh.shape["row"], mesh.shape["col"]
    planes = devices // 4
    row = ("half", "odd", "y", "core")
    parts = Mesh(mesh.devices.reshape(planes // 2, 2, 2, 2, columns), row + ("col",))

    def swap(value, flip):
        return lax.ppermute(value, row, [(i, i ^ flip) for i in range(devices)])

    def shards(vectors_in, householder, tfactors):
        odd, y, core = lax.axis_index("odd"), lax.axis_index("y"), lax.axis_index("core")
        z = lax.axis_index("half") * 2 + odd
        place = jnp.stack([z, y, core]).astype(jnp.int32)
        core = jnp.reshape(core, (1,)).astype(jnp.int32)
        each, length = vectors_in.shape
        wide = length // planes

        def moved(part, shift):
            return lax.ppermute(part, ("half", "odd"), [(i, (i + shift) % planes) for i in range(planes)])

        def sides(up, down, before):
            block = pltpu.VMEM((2, each, wide // 2), jnp.float32)
            return local_call(side_kernel, (block, block), [IN_VMEM, IN_VMEM, IN_HBM], (place, up, down, in_hbm(before)))

        def spread(kept, got):
            block = pltpu.VMEM((2, 2, each, wide // 4), jnp.float32)
            kept, sent = local_call(core_kernel, (block, block), [IN_VMEM, IN_VMEM], (place, kept, got))
            return kept, swap(sent, 1)

        block = pltpu.VMEM((each, wide), jnp.float32)
        cut = local_call(cut_kernel, (block,) * len(SHIFTS), [IN_HBM], (place, in_hbm(vectors_in)), len(SHIFTS))
        came = [moved(part, shift) for part, shift in zip(cut, SHIFTS)]
        packed = even_call(place, vectors_in, came[0], planes)
        even = lax.all_to_all(packed, ("half", "y", "core"), split_axis=0, concat_axis=0, tiled=True)
        one_kept, one_sent = sides(came[0], came[1], packed)
        one_got = swap(one_sent, 2)
        high, low, kept, sent = gram_call(core, householder, one_sent)
        gram = kept + swap(sent, 1)
        gram = gram + swap(gram, 2)
        three_kept, three_sent = sides(came[2], came[3], high)
        three_got = swap(three_sent, 2)
        scattered = spread(one_kept, one_got) + spread(three_kept, three_got)
        high = after(high, even)
        current, value, sent, gram = project_call(core, place, even, scattered, high, low, gram, swap(gram, 4))
        value = value + swap(sent, 1)
        value = value + swap(value, 2)
        half = value.shape[0]
        first, third = swap(value, 4), swap(value, 12)
        second = swap(jnp.concatenate([value, gram], axis=0), 8)
        own = jnp.concatenate([(value + first) + (second[:half] + third), gram + second[half:]], axis=0)
        own = own + swap(own, 24)
        other = swap(own, 1)
        return finish_call(core, own, other, tfactors, current, high, low)

    in_specs = (P(("col",) + row, None), P(None, None, row), P())
    out_specs = P("col", row)
    return jax.shard_map(shards, mesh=parts, in_specs=in_specs, out_specs=out_specs, check_vma=False)
```

```python
import functools

import jax
import jax.numpy as jnp
from jax import lax
from jax.experimental import pallas as pl
from jax.experimental.pallas import tpu as pltpu
from jax.sharding import Mesh
from jax.sharding import PartitionSpec as P

COLUMNS = 1024
OUT_COLUMNS = 2048
SHIFTS = (1, -1, 3, -3)
LIMIT = 40 * 1024 * 1024
IN_VMEM = pl.BlockSpec(memory_space=pltpu.VMEM)
IN_SMEM = pl.BlockSpec(memory_space=pltpu.SMEM)
IN_ANY = pl.BlockSpec(memory_space=pl.ANY)
IN_HBM = pl.BlockSpec(memory_space=pltpu.HBM)


def product(left, right, contract, precision=None):
    return lax.dot_general(
        left, right, (contract, ((), ())), precision=precision, preferred_element_type=jnp.float32
    )


def split(value):
    high = value.astype(jnp.bfloat16)
    low = (value - high.astype(jnp.float32)).astype(jnp.bfloat16)
    return high, low


def pairs_of(panels):
    return [(p, q) for p in range(panels) for q in range(p + 1, panels)]


def halves(core, whole, own_ref, other_ref):
    half = whole.shape[0] // 2
    own_ref[...] = whole[pl.ds(pl.multiple_of(core * half, 8), half), :]
    other_ref[...] = whole[pl.ds(pl.multiple_of((1 - core) * half, 8), half), :]


def gram_kernel(core_ref, householder_ref, before_ref, high_ref, low_ref, kept_ref, sent_ref, total, packed):
    del before_ref
    panels, width, columns = householder_ref.shape
    size = panels * width
    step = pl.program_id(0)

    @pl.when(step == 0)
    def _():
        total[...] = jnp.zeros_like(total)

    high, low = split(householder_ref[...].reshape(size, columns))
    high_ref[...] = high
    low_ref[...] = low
    both = jnp.concatenate([high, low], axis=0)
    first = product(both, high, ((1,), (1,)))
    second = product(both, low, ((1,), (1,)))
    total[...] += (first[:size] + first[size:]) + (second[:size] + second[size:])

    @pl.when(step == pl.num_programs(0) - 1)
    def _():
        blocks = [
            total[p * width : (p + 1) * width, q * width : (q + 1) * width] for p, q in pairs_of(panels)
        ]
        for i in range(0, len(blocks), 2):
            at = i // 2 * width
            packed[at : at + width, :] = jnp.concatenate(blocks[i : i + 2], axis=1)
        halves(core_ref[0], packed, kept_ref, sent_ref)


def cut_kernel(place_ref, vectors_ref, *refs):
    outs, sems = refs[:-1], refs[-1]
    wide = outs[0].shape[1]
    planes = vectors_ref.shape[1] // wide
    copies = []
    for i, shift in enumerate(SHIFTS):
        plane = (place_ref[0] + shift + planes) % planes
        columns = pl.ds(pl.multiple_of(plane * wide, 128), wide)
        copies.append(pltpu.make_async_copy(vectors_ref.at[:, columns], outs[i], sems.at[i]))
        copies[i].start()
    for copy in copies:
        copy.wait()


def even_kernel(place_ref, block_ref, before_ref, out_ref):
    del place_ref, before_ref
    number, _, wide = out_ref.shape
    for i in range(number):
        out_ref[i] = block_ref[:, i * wide : (i + 1) * wide]


def side_kernel(place_ref, up_ref, down_ref, before_ref, kept_ref, sent_ref):
    del before_ref
    wide = kept_ref.shape[2]
    y = place_ref[1]
    for i, part_ref in enumerate((up_ref, down_ref)):
        kept_ref[i] = part_ref[:, pl.ds(pl.multiple_of(y * wide, 128), wide)]
        sent_ref[i] = part_ref[:, pl.ds(pl.multiple_of((1 - y) * wide, 128), wide)]


def core_kernel(place_ref, own_ref, got_ref, kept_ref, sent_ref):
    wide = kept_ref.shape[3]
    core = place_ref[2]
    for i, part_ref in enumerate((own_ref, got_ref)):
        kept_ref[i] = part_ref[:, :, pl.ds(pl.multiple_of(core * wide, 128), wide)]
        sent_ref[i] = part_ref[:, :, pl.ds(pl.multiple_of((1 - core) * wide, 128), wide)]


def project_high_kernel(place_ref, even_ref, kept_one_ref, got_one_ref, kept_three_ref, got_three_ref, high_ref, current_ref, rounded_ref, total_ref):
    count, rows = current_ref.shape
    planes = count // (4 * even_ref.shape[1])
    z, y, core = place_ref[0], place_ref[1], place_ref[2]
    pair = 2 * even_ref.shape[1]
    total_ref[...] = jnp.zeros_like(total_ref)
    for step in range(rows // COLUMNS):
        columns = pl.ds(step * COLUMNS, COLUMNS)

        def put(plane, side, block):
            at = pl.multiple_of((plane * 2 + side) * pair, 8)
            current_ref[pl.ds(at, pair), columns] = block

        for k in range(planes // 2):
            for side in range(2):
                at = (2 * k + side) * 2
                put(2 * k + z % 2, side, even_ref[at : at + 2, :, columns].reshape(pair, COLUMNS))
        for shift, kept_ref, got_ref in ((1, kept_one_ref, got_one_ref), (3, kept_three_ref, got_three_ref)):
            for other in range(2):
                for i, by in enumerate((shift, -shift)):
                    kept, got = kept_ref[other, i, :, columns], got_ref[other, i, :, columns]
                    block = jnp.concatenate([jnp.where(core == 0, kept, got), jnp.where(core == 0, got, kept)], axis=0)
                    put((z - by + planes) % planes, y ^ other, block)
        high, low = split(current_ref[:, columns])
        rounded_ref[:, columns] = high
        both = jnp.concatenate([high, low], axis=0)
        total_ref[...] += product(high_ref[:, columns], both, ((1,), (1,)))


def after_kernel(held_ref, before_ref, same_ref):
    del held_ref, before_ref, same_ref


def project_low_kernel(core_ref, total_ref, rounded_ref, low_ref, gram_ref, more_ref, kept_ref, sent_ref, sum_ref, whole):
    sum_ref[...] = gram_ref[...] + more_ref[...]
    count = rounded_ref.shape[0]
    whole[...] = total_ref[:, :count] + (
        total_ref[:, count:] + product(low_ref[...], rounded_ref[...], ((1,), (1,)))
    )
    halves(core_ref[0], whole, kept_ref, sent_ref)


def finish_kernel(core_ref, own_ref, other_ref, tfactors_ref, current_ref, high_ref, low_ref, out_ref, joint, packed, out, sems):
    panels, width, _ = tfactors_ref.shape
    count, rows = current_ref.shape
    core = core_ref[0]
    half, rest = joint.shape[0] // 2, packed.shape[0] // 2
    for side, part_ref in ((core, own_ref), (1 - core, other_ref)):
        joint[pl.ds(pl.multiple_of(side * half, 8), half), :] = part_ref[:half, :]
        packed[pl.ds(pl.multiple_of(side * rest, 8), rest), :] = part_ref[half:, :]
    gram = {}
    for i, pair in enumerate(pairs_of(panels)):
        at = i // 2 * width
        gram[pair] = packed[at : at + width, i % 2 * width : (i % 2 + 1) * width]
    exact = functools.partial(product, contract=((1,), (0,)), precision=lax.Precision.HIGHEST)
    scaled = [exact(tfactors_ref[p], joint[p * width : (p + 1) * width, :]) for p in range(panels)]
    links = {(p, q): exact(tfactors_ref[p], gram[p, q]) for p, q in gram}
    for q in range(panels - 1, 0, -1):
        for p in range(q):
            scaled[p] = scaled[p] - exact(links[p, q], scaled[q])
    high, low = split(jnp.concatenate(scaled, axis=0).T)
    both = jnp.concatenate([high, low], axis=0)
    copies = []
    for step in range(rows // OUT_COLUMNS):
        columns = pl.ds(step * OUT_COLUMNS, OUT_COLUMNS)
        first = product(both, high_ref[:, columns], ((1,), (0,)))
        second = product(high, low_ref[:, columns], ((1,), (0,)))
        out[:, columns] = current_ref[:, columns] - (first[:count] + (first[count:] + second))
        copy = pltpu.make_async_copy(out.at[:, columns], out_ref.at[:, columns], sems.at[step])
        copy.start()
        copies.append(copy)
    for copy in copies:
        copy.wait()


def in_vmem(value):
    return pltpu.with_memory_space_constraint(value, pltpu.VMEM)


def in_hbm(value):
    return pltpu.with_memory_space_constraint(value, pltpu.HBM)


def gram_call(core, householder, before):
    panels, width, rows = householder.shape
    size = panels * width
    height = len(pairs_of(panels)) // 2 * width
    return pl.pallas_call(
        gram_kernel,
        out_shape=(
            pltpu.HBM((size, rows), jnp.bfloat16),
            pltpu.HBM((size, rows), jnp.bfloat16),
            jax.ShapeDtypeStruct((height // 2, 2 * width), jnp.float32),
            jax.ShapeDtypeStruct((height // 2, 2 * width), jnp.float32),
        ),
        grid=(rows // COLUMNS,),
        in_specs=[IN_SMEM, pl.BlockSpec((panels, width, COLUMNS), lambda i: (0, 0, i)), IN_ANY],
        out_specs=(
            pl.BlockSpec((size, COLUMNS), lambda i: (0, i)),
            pl.BlockSpec((size, COLUMNS), lambda i: (0, i)),
            pl.BlockSpec((height // 2, 2 * width), lambda i: (0, 0)),
            pl.BlockSpec((height // 2, 2 * width), lambda i: (0, 0)),
        ),
        scratch_shapes=[pltpu.VMEM((size, size), jnp.float32), pltpu.VMEM((height, 2 * width), jnp.float32)],
        compiler_params=pltpu.CompilerParams(vmem_limit_bytes=LIMIT),
        cost_estimate=pl.CostEstimate(flops=10 * 8 * size * size * rows, bytes_accessed=8 * size * rows, transcendentals=0),
        name="gram",
    )(core, in_hbm(householder), before)


def local_call(kernel, outs, specs, operands, copies=0):
    return pl.pallas_call(
        kernel,
        out_shape=outs,
        in_specs=[IN_SMEM] + specs,
        out_specs=tuple(IN_HBM if out.memory_space == pltpu.HBM else IN_VMEM for out in outs),
        scratch_shapes=[pltpu.SemaphoreType.DMA((copies,))] if copies else [],
        compiler_params=pltpu.CompilerParams(vmem_limit_bytes=LIMIT),
        name=kernel.__name__,
    )(*operands)


def even_call(place, vectors, before, planes):
    each, length = vectors.shape
    wide = length // planes
    return pl.pallas_call(
        even_kernel,
        out_shape=pltpu.HBM((planes * 2, each, wide // 4), jnp.float32),
        grid_spec=pltpu.PrefetchScalarGridSpec(
            num_scalar_prefetch=1,
            grid=(planes // 2,),
            in_specs=[pl.BlockSpec((each, wide), lambda k, place_ref: (0, 2 * k + place_ref[0] % 2)), IN_ANY],
            out_specs=pl.BlockSpec((4, each, wide // 4), lambda k, place_ref: (k, 0, 0)),
        ),
        compiler_params=pltpu.CompilerParams(vmem_limit_bytes=LIMIT),
        name="even",
    )(place, in_hbm(vectors), before)


def after(held, before):
    return pl.pallas_call(
        after_kernel,
        out_shape=pltpu.HBM(held.shape, held.dtype),
        in_specs=[IN_HBM, IN_ANY],
        out_specs=IN_HBM,
        input_output_aliases={0: 0},
        compiler_params=pltpu.CompilerParams(vmem_limit_bytes=1024 * 1024),
        name="after",
    )(in_hbm(held), before)


def project_call(core, place, even, odd, high, low, gram, more):
    sources, each, rows = even.shape
    count = 2 * sources * each
    size = high.shape[0]
    current, rounded, total = pl.pallas_call(
        project_high_kernel,
        out_shape=(
            pltpu.VMEM((count, rows), jnp.float32),
            pltpu.VMEM((count, rows), jnp.bfloat16),
            pltpu.VMEM((size, 2 * count), jnp.float32),
        ),
        in_specs=[IN_SMEM] + [IN_VMEM] * 6,
        out_specs=(IN_VMEM, IN_VMEM, IN_VMEM),
        compiler_params=pltpu.CompilerParams(vmem_limit_bytes=LIMIT),
        name="project_high",
    )(place, in_vmem(even), *[in_vmem(part) for part in odd], in_vmem(high))
    kept, sent, gram = pl.pallas_call(
        project_low_kernel,
        out_shape=(
            pltpu.VMEM((size // 2, count), jnp.float32),
            pltpu.VMEM((size // 2, count), jnp.float32),
            pltpu.VMEM(gram.shape, jnp.float32),
        ),
        in_specs=[IN_SMEM] + [IN_VMEM] * 5,
        out_specs=(IN_VMEM, IN_VMEM, IN_VMEM),
        scratch_shapes=[pltpu.VMEM((size, count), jnp.float32)],
        compiler_params=pltpu.CompilerParams(vmem_limit_bytes=LIMIT),
        name="project_low",
    )(core, in_vmem(total), in_vmem(rounded), in_vmem(low), in_vmem(gram), in_vmem(more))
    return current, kept, sent, gram


def finish_call(core, own, other, tfactors, current, high, low):
    count, rows = current.shape
    size = high.shape[0]
    return pl.pallas_call(
        finish_kernel,
        out_shape=jax.ShapeDtypeStruct((count, rows), jnp.float32),
        in_specs=[IN_SMEM] + [IN_VMEM] * 6,
        out_specs=IN_ANY,
        scratch_shapes=[
            pltpu.VMEM((size, count), jnp.float32),
            pltpu.VMEM((2 * own.shape[0] - size, count), jnp.float32),
            pltpu.VMEM((count, rows), jnp.float32),
            pltpu.SemaphoreType.DMA((rows // OUT_COLUMNS,)),
        ],
        compiler_params=pltpu.CompilerParams(vmem_limit_bytes=LIMIT),
        name="finish",
    )(core, in_vmem(own), in_vmem(other), tfactors, in_vmem(current), in_vmem(high), in_vmem(low))


def solution(mesh):
    devices, columns = mesh.shape["row"], mesh.shape["col"]
    planes = devices // 4
    row = ("half", "odd", "y", "core")
    parts = Mesh(mesh.devices.reshape(planes // 2, 2, 2, 2, columns), row + ("col",))

    def swap(value, flip):
        return lax.ppermute(value, row, [(i, i ^ flip) for i in range(devices)])

    def shards(vectors_in, householder, tfactors):
        odd, y, core = lax.axis_index("odd"), lax.axis_index("y"), lax.axis_index("core")
        z = lax.axis_index("half") * 2 + odd
        place = jnp.stack([z, y, core]).astype(jnp.int32)
        core = jnp.reshape(core, (1,)).astype(jnp.int32)
        each, length = vectors_in.shape
        wide = length // planes

        def moved(part, shift):
            return lax.ppermute(part, ("half", "odd"), [(i, (i + shift) % planes) for i in range(planes)])

        def spread(up, down, before):
            block = pltpu.VMEM((2, each, wide // 2), jnp.float32)
            kept, sent = local_call(side_kernel, (block, block), [IN_VMEM, IN_VMEM, IN_ANY], (place, up, down, before))
            block = pltpu.VMEM((2, 2, each, wide // 4), jnp.float32)
            kept, sent = local_call(core_kernel, (block, block), [IN_VMEM, IN_VMEM], (place, kept, swap(sent, 2)))
            return kept, swap(sent, 1)

        block = pltpu.VMEM((each, wide), jnp.float32)
        cut = local_call(cut_kernel, (block,) * len(SHIFTS), [IN_HBM], (place, in_hbm(vectors_in)), len(SHIFTS))
        came = [moved(part, shift) for part, shift in zip(cut, SHIFTS)]
        even = even_call(place, vectors_in, place, planes)
        even = lax.all_to_all(even, ("half", "y", "core"), split_axis=0, concat_axis=0, tiled=True)
        high, low, kept, sent = gram_call(core, householder, place)
        gram = kept + swap(sent, 1)
        gram = gram + swap(gram, 2)
        scattered = spread(came[0], came[1], kept) + spread(came[2], came[3], gram)
        high = after(high, even)
        current, value, sent, gram = project_call(core, place, even, scattered, high, low, gram, swap(gram, 4))
        value = value + swap(sent, 1)
        value = value + swap(value, 2)
        half = value.shape[0]
        first, third = swap(value, 4), swap(value, 12)
        second = swap(jnp.concatenate([value, gram], axis=0), 8)
        own = jnp.concatenate([(value + first) + (second[:half] + third), gram + second[half:]], axis=0)
        own = own + swap(own, 24)
        other = swap(own, 1)
        return finish_call(core, own, other, tfactors, current, high, low)

    in_specs = (P(("col",) + row, None), P(None, None, row), P())
    out_specs = P("col", row)
    return jax.shard_map(shards, mesh=parts, in_specs=in_specs, out_specs=out_specs, check_vma=False)
```

```python
import functools

import jax
import jax.numpy as jnp
from jax import lax
from jax.experimental import pallas as pl
from jax.experimental.pallas import tpu as pltpu
from jax.sharding import Mesh
from jax.sharding import PartitionSpec as P

COLUMNS = 1024
OUT_COLUMNS = 2048
NEAR, FAR = (1, -1), (3, -3)
LIMIT = 40 * 1024 * 1024
IN_VMEM = pl.BlockSpec(memory_space=pltpu.VMEM)
IN_SMEM = pl.BlockSpec(memory_space=pltpu.SMEM)
IN_ANY = pl.BlockSpec(memory_space=pl.ANY)
IN_HBM = pl.BlockSpec(memory_space=pltpu.HBM)


def product(left, right, contract, precision=None):
    return lax.dot_general(
        left, right, (contract, ((), ())), precision=precision, preferred_element_type=jnp.float32
    )


def split(value):
    high = value.astype(jnp.bfloat16)
    low = (value - high.astype(jnp.float32)).astype(jnp.bfloat16)
    return high, low


def pairs_of(panels):
    return [(p, q) for p in range(panels) for q in range(p + 1, panels)]


def halves(core, whole, own_ref, other_ref):
    half = whole.shape[0] // 2
    own_ref[...] = whole[pl.ds(pl.multiple_of(core * half, 8), half), :]
    other_ref[...] = whole[pl.ds(pl.multiple_of((1 - core) * half, 8), half), :]


def gram_kernel(core_ref, householder_ref, before_ref, high_ref, low_ref, kept_ref, sent_ref, total, packed):
    del before_ref
    panels, width, columns = householder_ref.shape
    size = panels * width
    step = pl.program_id(0)

    @pl.when(step == 0)
    def _():
        total[...] = jnp.zeros_like(total)

    high, low = split(householder_ref[...].reshape(size, columns))
    high_ref[...] = high
    low_ref[...] = low
    both = jnp.concatenate([high, low], axis=0)
    first = product(both, high, ((1,), (1,)))
    second = product(both, low, ((1,), (1,)))
    total[...] += (first[:size] + first[size:]) + (second[:size] + second[size:])

    @pl.when(step == pl.num_programs(0) - 1)
    def _():
        blocks = [
            total[p * width : (p + 1) * width, q * width : (q + 1) * width] for p, q in pairs_of(panels)
        ]
        for i in range(0, len(blocks), 2):
            at = i // 2 * width
            packed[at : at + width, :] = jnp.concatenate(blocks[i : i + 2], axis=1)
        halves(core_ref[0], packed, kept_ref, sent_ref)


def cut_kernel(shifts, place_ref, vectors_ref, *refs):
    outs, sems = refs[:-1], refs[-1]
    wide = outs[0].shape[1]
    planes = vectors_ref.shape[1] // wide
    copies = []
    for i, shift in enumerate(shifts):
        plane = (place_ref[0] + shift + planes) % planes
        columns = pl.ds(pl.multiple_of(plane * wide, 128), wide)
        copies.append(pltpu.make_async_copy(vectors_ref.at[:, columns], outs[i], sems.at[i]))
        copies[i].start()
    for copy in copies:
        copy.wait()


def even_kernel(place_ref, block_ref, before_ref, out_ref):
    del place_ref, before_ref
    number, _, wide = out_ref.shape
    for i in range(number):
        out_ref[i] = block_ref[:, i * wide : (i + 1) * wide]


def side_kernel(place_ref, up_ref, down_ref, before_ref, kept_ref, sent_ref):
    del before_ref
    wide = kept_ref.shape[2]
    y = place_ref[1]
    for i, part_ref in enumerate((up_ref, down_ref)):
        kept_ref[i] = part_ref[:, pl.ds(pl.multiple_of(y * wide, 128), wide)]
        sent_ref[i] = part_ref[:, pl.ds(pl.multiple_of((1 - y) * wide, 128), wide)]


def core_kernel(place_ref, own_ref, got_ref, kept_ref, sent_ref):
    wide = kept_ref.shape[3]
    core = place_ref[2]
    for i, part_ref in enumerate((own_ref, got_ref)):
        kept_ref[i] = part_ref[:, :, pl.ds(pl.multiple_of(core * wide, 128), wide)]
        sent_ref[i] = part_ref[:, :, pl.ds(pl.multiple_of((1 - core) * wide, 128), wide)]


def project_high_kernel(place_ref, even_ref, kept_one_ref, got_one_ref, kept_three_ref, got_three_ref, high_ref, current_ref, rounded_ref, total_ref):
    count, rows = current_ref.shape
    planes = count // (4 * even_ref.shape[1])
    z, y, core = place_ref[0], place_ref[1], place_ref[2]
    pair = 2 * even_ref.shape[1]
    total_ref[...] = jnp.zeros_like(total_ref)
    for step in range(rows // COLUMNS):
        columns = pl.ds(step * COLUMNS, COLUMNS)

        def put(plane, side, block):
            at = pl.multiple_of((plane * 2 + side) * pair, 8)
            current_ref[pl.ds(at, pair), columns] = block

        for k in range(planes // 2):
            for side in range(2):
                at = (2 * k + side) * 2
                put(2 * k + z % 2, side, even_ref[at : at + 2, :, columns].reshape(pair, COLUMNS))
        for shift, kept_ref, got_ref in ((1, kept_one_ref, got_one_ref), (3, kept_three_ref, got_three_ref)):
            for other in range(2):
                for i, by in enumerate((shift, -shift)):
                    kept, got = kept_ref[other, i, :, columns], got_ref[other, i, :, columns]
                    block = jnp.concatenate([jnp.where(core == 0, kept, got), jnp.where(core == 0, got, kept)], axis=0)
                    put((z - by + planes) % planes, y ^ other, block)
        high, low = split(current_ref[:, columns])
        rounded_ref[:, columns] = high
        both = jnp.concatenate([high, low], axis=0)
        total_ref[...] += product(high_ref[:, columns], both, ((1,), (1,)))


def after_kernel(held_ref, before_ref, same_ref):
    del held_ref, before_ref, same_ref


def project_low_kernel(core_ref, total_ref, rounded_ref, low_ref, gram_ref, more_ref, kept_ref, sent_ref, sum_ref, whole):
    sum_ref[...] = gram_ref[...] + more_ref[...]
    count = rounded_ref.shape[0]
    whole[...] = total_ref[:, :count] + (
        total_ref[:, count:] + product(low_ref[...], rounded_ref[...], ((1,), (1,)))
    )
    halves(core_ref[0], whole, kept_ref, sent_ref)


def finish_kernel(core_ref, own_ref, other_ref, tfactors_ref, current_ref, high_ref, low_ref, out_ref, joint, packed, out, sems):
    panels, width, _ = tfactors_ref.shape
    count, rows = current_ref.shape
    core = core_ref[0]
    half, rest = joint.shape[0] // 2, packed.shape[0] // 2
    for side, part_ref in ((core, own_ref), (1 - core, other_ref)):
        joint[pl.ds(pl.multiple_of(side * half, 8), half), :] = part_ref[:half, :]
        packed[pl.ds(pl.multiple_of(side * rest, 8), rest), :] = part_ref[half:, :]
    pairs = pairs_of(panels)
    exact = functools.partial(product, contract=((1,), (0,)), precision=lax.Precision.HIGHEST)
    scaled, links = [], {}
    for p in range(panels):
        tiles = sorted({i // 2 for i, pair in enumerate(pairs) if pair[0] == p})
        right = [joint[p * width : (p + 1) * width, :]] + [packed[i * width : (i + 1) * width, :] for i in tiles]
        whole = exact(tfactors_ref[p], jnp.concatenate(right, axis=1))
        scaled.append(whole[:, :count])
        for i, pair in enumerate(pairs):
            if pair[0] == p:
                at = count + tiles.index(i // 2) * 2 * width + i % 2 * width
                links[pair] = whole[:, at : at + width]
    for q in range(panels - 1, 0, -1):
        less = exact(jnp.concatenate([links[p, q] for p in range(q)], axis=0), scaled[q])
        for p in range(q):
            scaled[p] = scaled[p] - less[p * width : (p + 1) * width]
    high, low = split(jnp.concatenate(scaled, axis=0).T)
    both = jnp.concatenate([high, low], axis=0)
    copies = []
    for step in range(rows // OUT_COLUMNS):
        columns = pl.ds(step * OUT_COLUMNS, OUT_COLUMNS)
        first = product(both, high_ref[:, columns], ((1,), (0,)))
        second = product(high, low_ref[:, columns], ((1,), (0,)))
        out[:, columns] = current_ref[:, columns] - (first[:count] + (first[count:] + second))
        copy = pltpu.make_async_copy(out.at[:, columns], out_ref.at[:, columns], sems.at[step])
        copy.start()
        copies.append(copy)
    for copy in copies:
        copy.wait()


def in_vmem(value):
    return pltpu.with_memory_space_constraint(value, pltpu.VMEM)


def in_hbm(value):
    return pltpu.with_memory_space_constraint(value, pltpu.HBM)


def gram_call(core, householder, before):
    panels, width, rows = householder.shape
    size = panels * width
    height = len(pairs_of(panels)) // 2 * width
    return pl.pallas_call(
        gram_kernel,
        out_shape=(
            pltpu.HBM((size, rows), jnp.bfloat16),
            pltpu.HBM((size, rows), jnp.bfloat16),
            jax.ShapeDtypeStruct((height // 2, 2 * width), jnp.float32),
            jax.ShapeDtypeStruct((height // 2, 2 * width), jnp.float32),
        ),
        grid=(rows // COLUMNS,),
        in_specs=[IN_SMEM, pl.BlockSpec((panels, width, COLUMNS), lambda i: (0, 0, i)), IN_ANY],
        out_specs=(
            pl.BlockSpec((size, COLUMNS), lambda i: (0, i)),
            pl.BlockSpec((size, COLUMNS), lambda i: (0, i)),
            pl.BlockSpec((height // 2, 2 * width), lambda i: (0, 0)),
            pl.BlockSpec((height // 2, 2 * width), lambda i: (0, 0)),
        ),
        scratch_shapes=[pltpu.VMEM((size, size), jnp.float32), pltpu.VMEM((height, 2 * width), jnp.float32)],
        compiler_params=pltpu.CompilerParams(vmem_limit_bytes=LIMIT),
        cost_estimate=pl.CostEstimate(flops=10 * 8 * size * size * rows, bytes_accessed=8 * size * rows, transcendentals=0),
        name="gram",
    )(core, in_hbm(householder), before)


def local_call(kernel, outs, specs, operands, copies=0):
    return pl.pallas_call(
        kernel,
        out_shape=outs,
        in_specs=[IN_SMEM] + specs,
        out_specs=tuple(IN_HBM if out.memory_space == pltpu.HBM else IN_VMEM for out in outs),
        scratch_shapes=[pltpu.SemaphoreType.DMA((copies,))] if copies else [],
        compiler_params=pltpu.CompilerParams(vmem_limit_bytes=LIMIT),
        name=getattr(kernel, "__name__", "cut"),
    )(*operands)


def even_call(place, vectors, before, planes):
    each, length = vectors.shape
    wide = length // planes
    return pl.pallas_call(
        even_kernel,
        out_shape=pltpu.HBM((planes * 2, each, wide // 4), jnp.float32),
        grid_spec=pltpu.PrefetchScalarGridSpec(
            num_scalar_prefetch=1,
            grid=(planes // 2,),
            in_specs=[pl.BlockSpec((each, wide), lambda k, place_ref: (0, 2 * k + place_ref[0] % 2)), IN_ANY],
            out_specs=pl.BlockSpec((4, each, wide // 4), lambda k, place_ref: (k, 0, 0)),
        ),
        compiler_params=pltpu.CompilerParams(vmem_limit_bytes=LIMIT),
        name="even",
    )(place, in_hbm(vectors), before)


def after(held, before):
    return pl.pallas_call(
        after_kernel,
        out_shape=pltpu.HBM(held.shape, held.dtype),
        in_specs=[IN_HBM, IN_ANY],
        out_specs=IN_HBM,
        input_output_aliases={0: 0},
        compiler_params=pltpu.CompilerParams(vmem_limit_bytes=1024 * 1024),
        name="after",
    )(in_hbm(held), before)


def project_call(core, place, even, odd, high, low, gram, more):
    sources, each, rows = even.shape
    count = 2 * sources * each
    size = high.shape[0]
    current, rounded, total = pl.pallas_call(
        project_high_kernel,
        out_shape=(
            pltpu.VMEM((count, rows), jnp.float32),
            pltpu.VMEM((count, rows), jnp.bfloat16),
            pltpu.VMEM((size, 2 * count), jnp.float32),
        ),
        in_specs=[IN_SMEM] + [IN_VMEM] * 6,
        out_specs=(IN_VMEM, IN_VMEM, IN_VMEM),
        compiler_params=pltpu.CompilerParams(vmem_limit_bytes=LIMIT),
        name="project_high",
    )(place, in_vmem(even), *[in_vmem(part) for part in odd], in_vmem(high))
    kept, sent, gram = pl.pallas_call(
        project_low_kernel,
        out_shape=(
            pltpu.VMEM((size // 2, count), jnp.float32),
            pltpu.VMEM((size // 2, count), jnp.float32),
            pltpu.VMEM(gram.shape, jnp.float32),
        ),
        in_specs=[IN_SMEM] + [IN_VMEM] * 5,
        out_specs=(IN_VMEM, IN_VMEM, IN_VMEM),
        scratch_shapes=[pltpu.VMEM((size, count), jnp.float32)],
        compiler_params=pltpu.CompilerParams(vmem_limit_bytes=LIMIT),
        name="project_low",
    )(core, in_vmem(total), in_vmem(rounded), in_vmem(low), in_vmem(gram), in_vmem(more))
    return current, kept, sent, gram


def finish_call(core, own, other, tfactors, current, high, low):
    count, rows = current.shape
    size = high.shape[0]
    return pl.pallas_call(
        finish_kernel,
        out_shape=jax.ShapeDtypeStruct((count, rows), jnp.float32),
        in_specs=[IN_SMEM] + [IN_VMEM] * 6,
        out_specs=IN_ANY,
        scratch_shapes=[
            pltpu.VMEM((size, count), jnp.float32),
            pltpu.VMEM((2 * own.shape[0] - size, count), jnp.float32),
            pltpu.VMEM((count, rows), jnp.float32),
            pltpu.SemaphoreType.DMA((rows // OUT_COLUMNS,)),
        ],
        compiler_params=pltpu.CompilerParams(vmem_limit_bytes=LIMIT),
        name="finish",
    )(core, in_vmem(own), in_vmem(other), tfactors, in_vmem(current), in_vmem(high), in_vmem(low))


def solution(mesh):
    devices, columns = mesh.shape["row"], mesh.shape["col"]
    planes = devices // 4
    row = ("half", "odd", "y", "core")
    parts = Mesh(mesh.devices.reshape(planes // 2, 2, 2, 2, columns), row + ("col",))

    def swap(value, flip):
        return lax.ppermute(value, row, [(i, i ^ flip) for i in range(devices)])

    def shards(vectors_in, householder, tfactors):
        odd, y, core = lax.axis_index("odd"), lax.axis_index("y"), lax.axis_index("core")
        z = lax.axis_index("half") * 2 + odd
        place = jnp.stack([z, y, core]).astype(jnp.int32)
        core = jnp.reshape(core, (1,)).astype(jnp.int32)
        each, length = vectors_in.shape
        wide = length // planes

        def moved(part, shift):
            return lax.ppermute(part, ("half", "odd"), [(i, (i + shift) % planes) for i in range(planes)])

        def spread(up, down, before):
            block = pltpu.VMEM((2, each, wide // 2), jnp.float32)
            kept, sent = local_call(side_kernel, (block, block), [IN_VMEM, IN_VMEM, IN_ANY], (place, up, down, before))
            block = pltpu.VMEM((2, 2, each, wide // 4), jnp.float32)
            kept, sent = local_call(core_kernel, (block, block), [IN_VMEM, IN_VMEM], (place, kept, swap(sent, 2)))
            return kept, swap(sent, 1)

        block = pltpu.VMEM((each, wide), jnp.float32)
        came = []
        for shifts in (NEAR, FAR):
            kernel = functools.partial(cut_kernel, shifts)
            cut = local_call(kernel, (block,) * len(shifts), [IN_HBM], (place, in_hbm(vectors_in)), len(shifts))
            came += [moved(part, shift) for part, shift in zip(cut, shifts)]
        even = even_call(place, vectors_in, place, planes)
        even = lax.all_to_all(even, ("half", "y", "core"), split_axis=0, concat_axis=0, tiled=True)
        high, low, kept, sent = gram_call(core, householder, place)
        gram = kept + swap(sent, 1)
        gram = gram + swap(gram, 2)
        scattered = spread(came[0], came[1], kept) + spread(came[2], came[3], gram)
        high = after(high, even)
        current, value, sent, gram = project_call(core, place, even, scattered, high, low, gram, swap(gram, 4))
        value = value + swap(sent, 1)
        value = value + swap(value, 2)
        half = value.shape[0]
        first, third = swap(value, 4), swap(value, 12)
        second = swap(jnp.concatenate([value, gram], axis=0), 8)
        own = jnp.concatenate([(value + first) + (second[:half] + third), gram + second[half:]], axis=0)
        own = own + swap(own, 24)
        other = swap(own, 1)
        return finish_call(core, own, other, tfactors, current, high, low)

    in_specs = (P(("col",) + row, None), P(None, None, row), P())
    out_specs = P("col", row)
    return jax.shard_map(shards, mesh=parts, in_specs=in_specs, out_specs=out_specs, check_vma=False)
```

```python
import functools

import jax
import jax.numpy as jnp
from jax import lax
from jax.experimental import pallas as pl
from jax.experimental.pallas import tpu as pltpu
from jax.sharding import Mesh
from jax.sharding import PartitionSpec as P

COLUMNS = 1024
OUT_COLUMNS = 1024
WIDE_COLUMNS = 2048
NEAR, FAR = (1, -1), (3, -3)
LIMIT = 40 * 1024 * 1024
IN_VMEM = pl.BlockSpec(memory_space=pltpu.VMEM)
IN_SMEM = pl.BlockSpec(memory_space=pltpu.SMEM)
IN_ANY = pl.BlockSpec(memory_space=pl.ANY)
IN_HBM = pl.BlockSpec(memory_space=pltpu.HBM)


def product(left, right, contract, precision=None):
    return lax.dot_general(
        left, right, (contract, ((), ())), precision=precision, preferred_element_type=jnp.float32
    )


def split(value):
    high = value.astype(jnp.bfloat16)
    low = (value - high.astype(jnp.float32)).astype(jnp.bfloat16)
    return high, low


def pairs_of(panels):
    return [(p, q) for p in range(panels) for q in range(p + 1, panels)]


def halves(core, whole, own_ref, other_ref):
    half = whole.shape[0] // 2
    own_ref[...] = whole[pl.ds(pl.multiple_of(core * half, 8), half), :]
    other_ref[...] = whole[pl.ds(pl.multiple_of((1 - core) * half, 8), half), :]


def gram_kernel(core_ref, householder_ref, before_ref, high_ref, low_ref, kept_ref, sent_ref, total, packed):
    del before_ref
    panels, width, columns = householder_ref.shape
    size = panels * width
    step = pl.program_id(0)

    @pl.when(step == 0)
    def _():
        total[...] = jnp.zeros_like(total)

    high, low = split(householder_ref[...].reshape(size, columns))
    high_ref[...] = high
    low_ref[...] = low
    both = jnp.concatenate([high, low], axis=0)
    first = product(both, high, ((1,), (1,)))
    second = product(both, low, ((1,), (1,)))
    total[...] += (first[:size] + first[size:]) + (second[:size] + second[size:])

    @pl.when(step == pl.num_programs(0) - 1)
    def _():
        blocks = [
            total[p * width : (p + 1) * width, q * width : (q + 1) * width] for p, q in pairs_of(panels)
        ]
        for i in range(0, len(blocks), 2):
            at = i // 2 * width
            packed[at : at + width, :] = jnp.concatenate(blocks[i : i + 2], axis=1)
        halves(core_ref[0], packed, kept_ref, sent_ref)


def cut_kernel(shifts, place_ref, vectors_ref, *refs):
    outs, sems = refs[:-1], refs[-1]
    wide = outs[0].shape[1]
    planes = vectors_ref.shape[1] // wide
    copies = []
    for i, shift in enumerate(shifts):
        plane = (place_ref[0] + shift + planes) % planes
        columns = pl.ds(pl.multiple_of(plane * wide, 128), wide)
        copies.append(pltpu.make_async_copy(vectors_ref.at[:, columns], outs[i], sems.at[i]))
        copies[i].start()
    for copy in copies:
        copy.wait()


def even_kernel(place_ref, block_ref, before_ref, out_ref):
    del place_ref, before_ref
    number, _, wide = out_ref.shape
    for i in range(number):
        out_ref[i] = block_ref[:, i * wide : (i + 1) * wide]


def side_kernel(place_ref, up_ref, down_ref, before_ref, kept_ref, sent_ref):
    del before_ref
    wide = kept_ref.shape[2]
    y = place_ref[1]
    for i, part_ref in enumerate((up_ref, down_ref)):
        kept_ref[i] = part_ref[:, pl.ds(pl.multiple_of(y * wide, 128), wide)]
        sent_ref[i] = part_ref[:, pl.ds(pl.multiple_of((1 - y) * wide, 128), wide)]


def core_kernel(place_ref, own_ref, got_ref, kept_ref, sent_ref):
    wide = kept_ref.shape[3]
    core = place_ref[2]
    for i, part_ref in enumerate((own_ref, got_ref)):
        kept_ref[i] = part_ref[:, :, pl.ds(pl.multiple_of(core * wide, 128), wide)]
        sent_ref[i] = part_ref[:, :, pl.ds(pl.multiple_of((1 - core) * wide, 128), wide)]


def project_high_kernel(place_ref, even_ref, kept_one_ref, got_one_ref, kept_three_ref, got_three_ref, high_ref, current_ref, rounded_ref, total_ref):
    count, rows = current_ref.shape
    planes = count // (4 * even_ref.shape[1])
    z, y, core = place_ref[0], place_ref[1], place_ref[2]
    pair = 2 * even_ref.shape[1]
    total_ref[...] = jnp.zeros_like(total_ref)
    for step in range(rows // WIDE_COLUMNS):
        columns = pl.ds(step * WIDE_COLUMNS, WIDE_COLUMNS)

        def put(plane, side, block):
            at = pl.multiple_of((plane * 2 + side) * pair, 8)
            current_ref[pl.ds(at, pair), columns] = block

        for k in range(planes // 2):
            for side in range(2):
                at = (2 * k + side) * 2
                put(2 * k + z % 2, side, even_ref[at : at + 2, :, columns].reshape(pair, WIDE_COLUMNS))
        for shift, kept_ref, got_ref in ((1, kept_one_ref, got_one_ref), (3, kept_three_ref, got_three_ref)):
            for other in range(2):
                for i, by in enumerate((shift, -shift)):
                    kept, got = kept_ref[other, i, :, columns], got_ref[other, i, :, columns]
                    block = jnp.concatenate([jnp.where(core == 0, kept, got), jnp.where(core == 0, got, kept)], axis=0)
                    put((z - by + planes) % planes, y ^ other, block)
        high, low = split(current_ref[:, columns])
        rounded_ref[:, columns] = high
        both = jnp.concatenate([high, low], axis=0)
        total_ref[...] += product(high_ref[:, columns], both, ((1,), (1,)))


def after_kernel(held_ref, before_ref, same_ref):
    del held_ref, before_ref, same_ref


def project_low_kernel(core_ref, total_ref, rounded_ref, low_ref, gram_ref, more_ref, kept_ref, sent_ref, sum_ref, whole):
    sum_ref[...] = gram_ref[...] + more_ref[...]
    count = rounded_ref.shape[0]
    whole[...] = total_ref[:, :count] + (
        total_ref[:, count:] + product(low_ref[...], rounded_ref[...], ((1,), (1,)))
    )
    halves(core_ref[0], whole, kept_ref, sent_ref)


def finish_kernel(core_ref, own_ref, other_ref, tfactors_ref, current_ref, high_ref, low_ref, out_ref, joint, packed, out, sems):
    panels, width, _ = tfactors_ref.shape
    count, rows = current_ref.shape
    core = core_ref[0]
    half, rest = joint.shape[0] // 2, packed.shape[0] // 2
    for side, part_ref in ((core, own_ref), (1 - core, other_ref)):
        joint[pl.ds(pl.multiple_of(side * half, 8), half), :] = part_ref[:half, :]
        packed[pl.ds(pl.multiple_of(side * rest, 8), rest), :] = part_ref[half:, :]
    gram = {}
    for i, pair in enumerate(pairs_of(panels)):
        at = i // 2 * width
        gram[pair] = packed[at : at + width, i % 2 * width : (i % 2 + 1) * width]
    exact = functools.partial(product, contract=((1,), (0,)), precision=lax.Precision.HIGHEST)
    scaled = [exact(tfactors_ref[p], joint[p * width : (p + 1) * width, :]) for p in range(panels)]
    links = {(p, q): exact(tfactors_ref[p], gram[p, q]) for p, q in gram}
    for q in range(panels - 1, 0, -1):
        for p in range(q):
            scaled[p] = scaled[p] - exact(links[p, q], scaled[q])
    high, low = split(jnp.concatenate(scaled, axis=0).T)
    both = jnp.concatenate([high, low], axis=0)
    copies = []
    for step in range(rows // OUT_COLUMNS):
        columns = pl.ds(step * OUT_COLUMNS, OUT_COLUMNS)
        first = product(both, high_ref[:, columns], ((1,), (0,)))
        second = product(high, low_ref[:, columns], ((1,), (0,)))
        out[:, columns] = current_ref[:, columns] - (first[:count] + (first[count:] + second))
        copy = pltpu.make_async_copy(out.at[:, columns], out_ref.at[:, columns], sems.at[step])
        copy.start()
        copies.append(copy)
    for copy in copies:
        copy.wait()


def in_vmem(value):
    return pltpu.with_memory_space_constraint(value, pltpu.VMEM)


def in_hbm(value):
    return pltpu.with_memory_space_constraint(value, pltpu.HBM)


def gram_call(core, householder, before):
    panels, width, rows = householder.shape
    size = panels * width
    height = len(pairs_of(panels)) // 2 * width
    return pl.pallas_call(
        gram_kernel,
        out_shape=(
            pltpu.HBM((size, rows), jnp.bfloat16),
            pltpu.HBM((size, rows), jnp.bfloat16),
            jax.ShapeDtypeStruct((height // 2, 2 * width), jnp.float32),
            jax.ShapeDtypeStruct((height // 2, 2 * width), jnp.float32),
        ),
        grid=(rows // COLUMNS,),
        in_specs=[IN_SMEM, pl.BlockSpec((panels, width, COLUMNS), lambda i: (0, 0, i)), IN_ANY],
        out_specs=(
            pl.BlockSpec((size, COLUMNS), lambda i: (0, i)),
            pl.BlockSpec((size, COLUMNS), lambda i: (0, i)),
            pl.BlockSpec((height // 2, 2 * width), lambda i: (0, 0)),
            pl.BlockSpec((height // 2, 2 * width), lambda i: (0, 0)),
        ),
        scratch_shapes=[pltpu.VMEM((size, size), jnp.float32), pltpu.VMEM((height, 2 * width), jnp.float32)],
        compiler_params=pltpu.CompilerParams(vmem_limit_bytes=LIMIT),
        cost_estimate=pl.CostEstimate(flops=10 * 8 * size * size * rows, bytes_accessed=8 * size * rows, transcendentals=0),
        name="gram",
    )(core, in_hbm(householder), before)


def local_call(kernel, outs, specs, operands, copies=0):
    return pl.pallas_call(
        kernel,
        out_shape=outs,
        in_specs=[IN_SMEM] + specs,
        out_specs=tuple(IN_HBM if out.memory_space == pltpu.HBM else IN_VMEM for out in outs),
        scratch_shapes=[pltpu.SemaphoreType.DMA((copies,))] if copies else [],
        compiler_params=pltpu.CompilerParams(vmem_limit_bytes=LIMIT),
        name=getattr(kernel, "__name__", "cut"),
    )(*operands)


def even_call(place, vectors, before, planes):
    each, length = vectors.shape
    wide = length // planes
    return pl.pallas_call(
        even_kernel,
        out_shape=pltpu.HBM((planes * 2, each, wide // 4), jnp.float32),
        grid_spec=pltpu.PrefetchScalarGridSpec(
            num_scalar_prefetch=1,
            grid=(planes // 2,),
            in_specs=[pl.BlockSpec((each, wide), lambda k, place_ref: (0, 2 * k + place_ref[0] % 2)), IN_ANY],
            out_specs=pl.BlockSpec((4, each, wide // 4), lambda k, place_ref: (k, 0, 0)),
        ),
        compiler_params=pltpu.CompilerParams(vmem_limit_bytes=LIMIT),
        name="even",
    )(place, in_hbm(vectors), before)


def after(held, before):
    return pl.pallas_call(
        after_kernel,
        out_shape=pltpu.HBM(held.shape, held.dtype),
        in_specs=[IN_HBM, IN_ANY],
        out_specs=IN_HBM,
        input_output_aliases={0: 0},
        compiler_params=pltpu.CompilerParams(vmem_limit_bytes=1024 * 1024),
        name="after",
    )(in_hbm(held), before)


def project_call(core, place, even, odd, high, low, gram, more):
    sources, each, rows = even.shape
    count = 2 * sources * each
    size = high.shape[0]
    current, rounded, total = pl.pallas_call(
        project_high_kernel,
        out_shape=(
            pltpu.VMEM((count, rows), jnp.float32),
            pltpu.VMEM((count, rows), jnp.bfloat16),
            pltpu.VMEM((size, 2 * count), jnp.float32),
        ),
        in_specs=[IN_SMEM] + [IN_VMEM] * 6,
        out_specs=(IN_VMEM, IN_VMEM, IN_VMEM),
        compiler_params=pltpu.CompilerParams(vmem_limit_bytes=LIMIT),
        name="project_high",
    )(place, in_vmem(even), *[in_vmem(part) for part in odd], in_vmem(high))
    kept, sent, gram = pl.pallas_call(
        project_low_kernel,
        out_shape=(
            pltpu.VMEM((size // 2, count), jnp.float32),
            pltpu.VMEM((size // 2, count), jnp.float32),
            pltpu.VMEM(gram.shape, jnp.float32),
        ),
        in_specs=[IN_SMEM] + [IN_VMEM] * 5,
        out_specs=(IN_VMEM, IN_VMEM, IN_VMEM),
        scratch_shapes=[pltpu.VMEM((size, count), jnp.float32)],
        compiler_params=pltpu.CompilerParams(vmem_limit_bytes=LIMIT),
        name="project_low",
    )(core, in_vmem(total), in_vmem(rounded), in_vmem(low), in_vmem(gram), in_vmem(more))
    return current, kept, sent, gram


def finish_call(core, own, other, tfactors, current, high, low):
    count, rows = current.shape
    size = high.shape[0]
    return pl.pallas_call(
        finish_kernel,
        out_shape=jax.ShapeDtypeStruct((count, rows), jnp.float32),
        in_specs=[IN_SMEM] + [IN_VMEM] * 6,
        out_specs=IN_ANY,
        scratch_shapes=[
            pltpu.VMEM((size, count), jnp.float32),
            pltpu.VMEM((2 * own.shape[0] - size, count), jnp.float32),
            pltpu.VMEM((count, rows), jnp.float32),
            pltpu.SemaphoreType.DMA((rows // OUT_COLUMNS,)),
        ],
        compiler_params=pltpu.CompilerParams(vmem_limit_bytes=LIMIT),
        name="finish",
    )(core, in_vmem(own), in_vmem(other), tfactors, in_vmem(current), in_vmem(high), in_vmem(low))


def solution(mesh):
    devices, columns = mesh.shape["row"], mesh.shape["col"]
    planes = devices // 4
    row = ("half", "odd", "y", "core")
    parts = Mesh(mesh.devices.reshape(planes // 2, 2, 2, 2, columns), row + ("col",))

    def swap(value, flip):
        return lax.ppermute(value, row, [(i, i ^ flip) for i in range(devices)])

    def shards(vectors_in, householder, tfactors):
        odd, y, core = lax.axis_index("odd"), lax.axis_index("y"), lax.axis_index("core")
        z = lax.axis_index("half") * 2 + odd
        place = jnp.stack([z, y, core]).astype(jnp.int32)
        core = jnp.reshape(core, (1,)).astype(jnp.int32)
        each, length = vectors_in.shape
        wide = length // planes

        def moved(part, shift):
            return lax.ppermute(part, ("half", "odd"), [(i, (i + shift) % planes) for i in range(planes)])

        def spread(up, down, before):
            block = pltpu.VMEM((2, each, wide // 2), jnp.float32)
            kept, sent = local_call(side_kernel, (block, block), [IN_VMEM, IN_VMEM, IN_ANY], (place, up, down, before))
            block = pltpu.VMEM((2, 2, each, wide // 4), jnp.float32)
            kept, sent = local_call(core_kernel, (block, block), [IN_VMEM, IN_VMEM], (place, kept, swap(sent, 2)))
            return kept, swap(sent, 1)

        block = pltpu.VMEM((each, wide), jnp.float32)
        came = []
        for shifts in (NEAR, FAR):
            kernel = functools.partial(cut_kernel, shifts)
            cut = local_call(kernel, (block,) * len(shifts), [IN_HBM], (place, in_hbm(vectors_in)), len(shifts))
            came += [moved(part, shift) for part, shift in zip(cut, shifts)]
        even = even_call(place, vectors_in, place, planes)
        even = lax.all_to_all(even, ("half", "y", "core"), split_axis=0, concat_axis=0, tiled=True)
        high, low, kept, sent = gram_call(core, householder, place)
        gram = kept + swap(sent, 1)
        gram = gram + swap(gram, 2)
        scattered = spread(came[0], came[1], kept) + spread(came[2], came[3], gram)
        high = after(high, even)
        current, value, sent, gram = project_call(core, place, even, scattered, high, low, gram, swap(gram, 4))
        value = value + swap(sent, 1)
        value = value + swap(value, 2)
        half = value.shape[0]
        first, third = swap(value, 4), swap(value, 12)
        second = swap(jnp.concatenate([value, gram], axis=0), 8)
        own = jnp.concatenate([(value + first) + (second[:half] + third), gram + second[half:]], axis=0)
        own = own + swap(own, 24)
        other = swap(own, 1)
        return finish_call(core, own, other, tfactors, current, high, low)

    in_specs = (P(("col",) + row, None), P(None, None, row), P())
    out_specs = P("col", row)
    return jax.shard_map(shards, mesh=parts, in_specs=in_specs, out_specs=out_specs, check_vma=False)
```

```python
import functools

import jax
import jax.numpy as jnp
from jax import lax
from jax.experimental import pallas as pl
from jax.experimental.pallas import tpu as pltpu
from jax.sharding import Mesh
from jax.sharding import PartitionSpec as P

COLUMNS = 1024
OUT_COLUMNS = 2048
NEAR, FAR = (1, -1), (3, -3)
LIMIT = 40 * 1024 * 1024
IN_VMEM = pl.BlockSpec(memory_space=pltpu.VMEM)
IN_SMEM = pl.BlockSpec(memory_space=pltpu.SMEM)
IN_ANY = pl.BlockSpec(memory_space=pl.ANY)
IN_HBM = pl.BlockSpec(memory_space=pltpu.HBM)


def product(left, right, contract, precision=None):
    return lax.dot_general(
        left, right, (contract, ((), ())), precision=precision, preferred_element_type=jnp.float32
    )


def split(value):
    high = value.astype(jnp.bfloat16)
    low = (value - high.astype(jnp.float32)).astype(jnp.bfloat16)
    return high, low


def pairs_of(panels):
    return [(p, q) for p in range(panels) for q in range(p + 1, panels)]


def halves(core, whole, own_ref, other_ref):
    half = whole.shape[0] // 2
    own_ref[...] = whole[pl.ds(pl.multiple_of(core * half, 8), half), :]
    other_ref[...] = whole[pl.ds(pl.multiple_of((1 - core) * half, 8), half), :]


def gram_kernel(core_ref, householder_ref, before_ref, high_ref, low_ref, kept_ref, sent_ref, total, packed):
    del before_ref
    panels, width, columns = householder_ref.shape
    size = panels * width
    step = pl.program_id(0)

    @pl.when(step == 0)
    def _():
        total[...] = jnp.zeros_like(total)

    high, low = split(householder_ref[...].reshape(size, columns))
    high_ref[...] = high
    low_ref[...] = low
    both = jnp.concatenate([high, low], axis=0)
    first = product(both, high, ((1,), (1,)))
    second = product(both, low, ((1,), (1,)))
    total[...] += (first[:size] + first[size:]) + (second[:size] + second[size:])

    @pl.when(step == pl.num_programs(0) - 1)
    def _():
        blocks = [
            total[p * width : (p + 1) * width, q * width : (q + 1) * width] for p, q in pairs_of(panels)
        ]
        for i in range(0, len(blocks), 2):
            at = i // 2 * width
            packed[at : at + width, :] = jnp.concatenate(blocks[i : i + 2], axis=1)
        halves(core_ref[0], packed, kept_ref, sent_ref)


def cut_kernel(shifts, place_ref, vectors_ref, *refs):
    outs, sems = refs[:-1], refs[-1]
    wide = outs[0].shape[1]
    planes = vectors_ref.shape[1] // wide
    copies = []
    for i, shift in enumerate(shifts):
        plane = (place_ref[0] + shift + planes) % planes
        columns = pl.ds(pl.multiple_of(plane * wide, 128), wide)
        copies.append(pltpu.make_async_copy(vectors_ref.at[:, columns], outs[i], sems.at[i]))
        copies[i].start()
    for copy in copies:
        copy.wait()


def even_kernel(place_ref, block_ref, before_ref, out_ref):
    del place_ref, before_ref
    number, _, wide = out_ref.shape
    for i in range(number):
        out_ref[i] = block_ref[:, i * wide : (i + 1) * wide]


def side_kernel(place_ref, up_ref, down_ref, before_ref, kept_ref, sent_ref):
    del before_ref
    wide = kept_ref.shape[2]
    y = place_ref[1]
    for i, part_ref in enumerate((up_ref, down_ref)):
        kept_ref[i] = part_ref[:, pl.ds(pl.multiple_of(y * wide, 128), wide)]
        sent_ref[i] = part_ref[:, pl.ds(pl.multiple_of((1 - y) * wide, 128), wide)]


def core_kernel(place_ref, own_ref, got_ref, kept_ref, sent_ref):
    wide = kept_ref.shape[3]
    core = place_ref[2]
    for i, part_ref in enumerate((own_ref, got_ref)):
        kept_ref[i] = part_ref[:, :, pl.ds(pl.multiple_of(core * wide, 128), wide)]
        sent_ref[i] = part_ref[:, :, pl.ds(pl.multiple_of((1 - core) * wide, 128), wide)]


def project_high_kernel(place_ref, even_ref, kept_one_ref, got_one_ref, kept_three_ref, got_three_ref, high_ref, current_ref, rounded_ref, total_ref):
    count, rows = current_ref.shape
    planes = count // (4 * even_ref.shape[1])
    z, y, core = place_ref[0], place_ref[1], place_ref[2]
    pair = 2 * even_ref.shape[1]
    total_ref[...] = jnp.zeros_like(total_ref)
    for step in range(rows // COLUMNS):
        columns = pl.ds(step * COLUMNS, COLUMNS)

        def put(plane, side, block):
            at = pl.multiple_of((plane * 2 + side) * pair, 8)
            current_ref[pl.ds(at, pair), columns] = block

        for k in range(planes // 2):
            for side in range(2):
                at = (2 * k + side) * 2
                put(2 * k + z % 2, side, even_ref[at : at + 2, :, columns].reshape(pair, COLUMNS))
        for shift, kept_ref, got_ref in ((1, kept_one_ref, got_one_ref), (3, kept_three_ref, got_three_ref)):
            for other in range(2):
                for i, by in enumerate((shift, -shift)):
                    kept, got = kept_ref[other, i, :, columns], got_ref[other, i, :, columns]
                    block = jnp.concatenate([jnp.where(core == 0, kept, got), jnp.where(core == 0, got, kept)], axis=0)
                    put((z - by + planes) % planes, y ^ other, block)
        high, low = split(current_ref[:, columns])
        rounded_ref[:, columns] = high
        both = jnp.concatenate([high, low], axis=0)
        total_ref[...] += product(high_ref[:, columns], both, ((1,), (1,)))


def after_kernel(held_ref, before_ref, same_ref):
    del held_ref, before_ref, same_ref


def project_low_kernel(core_ref, total_ref, rounded_ref, low_ref, gram_ref, more_ref, kept_ref, sent_ref, sum_ref, whole):
    sum_ref[...] = gram_ref[...] + more_ref[...]
    count = rounded_ref.shape[0]
    whole[...] = total_ref[:, :count] + (
        total_ref[:, count:] + product(low_ref[...], rounded_ref[...], ((1,), (1,)))
    )
    halves(core_ref[0], whole, kept_ref, sent_ref)


def finish_kernel(core_ref, own_ref, other_ref, tfactors_ref, current_ref, high_ref, low_ref, out_ref, joint, packed, out, sems):
    panels, width, _ = tfactors_ref.shape
    count, rows = current_ref.shape
    core = core_ref[0]
    half, rest = joint.shape[0] // 2, packed.shape[0] // 2
    for side, part_ref in ((core, own_ref), (1 - core, other_ref)):
        joint[pl.ds(pl.multiple_of(side * half, 8), half), :] = part_ref[:half, :]
        packed[pl.ds(pl.multiple_of(side * rest, 8), rest), :] = part_ref[half:, :]
    pairs = pairs_of(panels)
    exact = functools.partial(product, contract=((1,), (0,)), precision=lax.Precision.HIGHEST)
    scaled, links = [], {}
    for p in range(panels):
        tiles = sorted({i // 2 for i, pair in enumerate(pairs) if pair[0] == p})
        right = [joint[p * width : (p + 1) * width, :]] + [packed[i * width : (i + 1) * width, :] for i in tiles]
        whole = exact(tfactors_ref[p], jnp.concatenate(right, axis=1))
        scaled.append(whole[:, :count])
        for i, pair in enumerate(pairs):
            if pair[0] == p:
                at = count + tiles.index(i // 2) * 2 * width + i % 2 * width
                links[pair] = whole[:, at : at + width]
    for q in range(panels - 1, 0, -1):
        less = exact(jnp.concatenate([links[p, q] for p in range(q)], axis=0), scaled[q])
        for p in range(q):
            scaled[p] = scaled[p] - less[p * width : (p + 1) * width]
    high, low = split(jnp.concatenate(scaled, axis=0).T)
    both = jnp.concatenate([high, low], axis=0)
    copies = []
    for step in range(rows // OUT_COLUMNS):
        columns = pl.ds(step * OUT_COLUMNS, OUT_COLUMNS)
        first = product(both, high_ref[:, columns], ((1,), (0,)))
        second = product(high, low_ref[:, columns], ((1,), (0,)))
        out[:, columns] = current_ref[:, columns] - (first[:count] + (first[count:] + second))
        copy = pltpu.make_async_copy(out.at[:, columns], out_ref.at[:, columns], sems.at[step])
        copy.start()
        copies.append(copy)
    for copy in copies:
        copy.wait()


def in_vmem(value):
    return pltpu.with_memory_space_constraint(value, pltpu.VMEM)


def in_hbm(value):
    return pltpu.with_memory_space_constraint(value, pltpu.HBM)


def gram_call(core, householder, before):
    panels, width, rows = householder.shape
    size = panels * width
    height = len(pairs_of(panels)) // 2 * width
    return pl.pallas_call(
        gram_kernel,
        out_shape=(
            pltpu.HBM((size, rows), jnp.bfloat16),
            pltpu.HBM((size, rows), jnp.bfloat16),
            jax.ShapeDtypeStruct((height // 2, 2 * width), jnp.float32),
            jax.ShapeDtypeStruct((height // 2, 2 * width), jnp.float32),
        ),
        grid=(rows // COLUMNS,),
        in_specs=[IN_SMEM, pl.BlockSpec((panels, width, COLUMNS), lambda i: (0, 0, i)), IN_ANY],
        out_specs=(
            pl.BlockSpec((size, COLUMNS), lambda i: (0, i)),
            pl.BlockSpec((size, COLUMNS), lambda i: (0, i)),
            pl.BlockSpec((height // 2, 2 * width), lambda i: (0, 0)),
            pl.BlockSpec((height // 2, 2 * width), lambda i: (0, 0)),
        ),
        scratch_shapes=[pltpu.VMEM((size, size), jnp.float32), pltpu.VMEM((height, 2 * width), jnp.float32)],
        compiler_params=pltpu.CompilerParams(vmem_limit_bytes=LIMIT),
        cost_estimate=pl.CostEstimate(flops=10 * 8 * size * size * rows, bytes_accessed=8 * size * rows, transcendentals=0),
        name="gram",
    )(core, in_hbm(householder), before)


def local_call(kernel, outs, specs, operands, copies=0):
    return pl.pallas_call(
        kernel,
        out_shape=outs,
        in_specs=[IN_SMEM] + specs,
        out_specs=tuple(IN_HBM if out.memory_space == pltpu.HBM else IN_VMEM for out in outs),
        scratch_shapes=[pltpu.SemaphoreType.DMA((copies,))] if copies else [],
        compiler_params=pltpu.CompilerParams(vmem_limit_bytes=LIMIT),
        name=getattr(kernel, "__name__", "cut"),
    )(*operands)


def even_call(place, vectors, before, planes):
    each, length = vectors.shape
    wide = length // planes
    return pl.pallas_call(
        even_kernel,
        out_shape=pltpu.HBM((planes * 2, each, wide // 4), jnp.float32),
        grid_spec=pltpu.PrefetchScalarGridSpec(
            num_scalar_prefetch=1,
            grid=(planes // 2,),
            in_specs=[pl.BlockSpec((each, wide), lambda k, place_ref: (0, 2 * k + place_ref[0] % 2)), IN_ANY],
            out_specs=pl.BlockSpec((4, each, wide // 4), lambda k, place_ref: (k, 0, 0)),
        ),
        compiler_params=pltpu.CompilerParams(vmem_limit_bytes=LIMIT),
        name="even",
    )(place, in_hbm(vectors), before)


def after(held, before):
    return pl.pallas_call(
        after_kernel,
        out_shape=pltpu.HBM(held.shape, held.dtype),
        in_specs=[IN_HBM, IN_ANY],
        out_specs=IN_HBM,
        input_output_aliases={0: 0},
        compiler_params=pltpu.CompilerParams(vmem_limit_bytes=1024 * 1024),
        name="after",
    )(in_hbm(held), before)


def project_call(core, place, even, odd, high, low, gram, more):
    sources, each, rows = even.shape
    count = 2 * sources * each
    size = high.shape[0]
    current, rounded, total = pl.pallas_call(
        project_high_kernel,
        out_shape=(
            pltpu.VMEM((count, rows), jnp.float32),
            pltpu.VMEM((count, rows), jnp.bfloat16),
            pltpu.VMEM((size, 2 * count), jnp.float32),
        ),
        in_specs=[IN_SMEM] + [IN_VMEM] * 6,
        out_specs=(IN_VMEM, IN_VMEM, IN_VMEM),
        compiler_params=pltpu.CompilerParams(vmem_limit_bytes=LIMIT),
        name="project_high",
    )(place, in_vmem(even), *[in_vmem(part) for part in odd], in_vmem(high))
    kept, sent, gram = pl.pallas_call(
        project_low_kernel,
        out_shape=(
            pltpu.VMEM((size // 2, count), jnp.float32),
            pltpu.VMEM((size // 2, count), jnp.float32),
            pltpu.VMEM(gram.shape, jnp.float32),
        ),
        in_specs=[IN_SMEM] + [IN_VMEM] * 5,
        out_specs=(IN_VMEM, IN_VMEM, IN_VMEM),
        scratch_shapes=[pltpu.VMEM((size, count), jnp.float32)],
        compiler_params=pltpu.CompilerParams(vmem_limit_bytes=LIMIT),
        name="project_low",
    )(core, in_vmem(total), in_vmem(rounded), in_vmem(low), in_vmem(gram), in_vmem(more))
    return current, kept, sent, gram


def finish_call(core, own, other, tfactors, current, high, low):
    count, rows = current.shape
    size = high.shape[0]
    return pl.pallas_call(
        finish_kernel,
        out_shape=jax.ShapeDtypeStruct((count, rows), jnp.float32),
        in_specs=[IN_SMEM] + [IN_VMEM] * 6,
        out_specs=IN_ANY,
        scratch_shapes=[
            pltpu.VMEM((size, count), jnp.float32),
            pltpu.VMEM((2 * own.shape[0] - size, count), jnp.float32),
            pltpu.VMEM((count, rows), jnp.float32),
            pltpu.SemaphoreType.DMA((rows // OUT_COLUMNS,)),
        ],
        compiler_params=pltpu.CompilerParams(vmem_limit_bytes=LIMIT),
        name="finish",
    )(core, in_vmem(own), in_vmem(other), tfactors, in_vmem(current), in_vmem(high), in_vmem(low))


def solution(mesh):
    devices, columns = mesh.shape["row"], mesh.shape["col"]
    planes = devices // 4
    row = ("half", "odd", "y", "core")
    parts = Mesh(mesh.devices.reshape(planes // 2, 2, 2, 2, columns), row + ("col",))

    def swap(value, flip):
        return lax.ppermute(value, row, [(i, i ^ flip) for i in range(devices)])

    def shards(vectors_in, householder, tfactors):
        odd, y, core = lax.axis_index("odd"), lax.axis_index("y"), lax.axis_index("core")
        z = lax.axis_index("half") * 2 + odd
        place = jnp.stack([z, y, core]).astype(jnp.int32)
        core = jnp.reshape(core, (1,)).astype(jnp.int32)
        each, length = vectors_in.shape
        wide = length // planes

        def moved(part, shift):
            return lax.ppermute(part, ("half", "odd"), [(i, (i + shift) % planes) for i in range(planes)])

        def spread(up, down, before):
            block = pltpu.VMEM((2, each, wide // 2), jnp.float32)
            kept, sent = local_call(side_kernel, (block, block), [IN_VMEM, IN_VMEM, IN_ANY], (place, up, down, before))
            block = pltpu.VMEM((2, 2, each, wide // 4), jnp.float32)
            kept, sent = local_call(core_kernel, (block, block), [IN_VMEM, IN_VMEM], (place, kept, swap(sent, 2)))
            return kept, swap(sent, 1)

        block = pltpu.VMEM((each, wide), jnp.float32)
        came = []
        for shifts in (NEAR, FAR):
            kernel = functools.partial(cut_kernel, shifts)
            cut = local_call(kernel, (block,) * len(shifts), [IN_HBM], (place, in_hbm(vectors_in)), len(shifts))
            came += [moved(part, shift) for part, shift in zip(cut, shifts)]
        even = even_call(place, vectors_in, place, planes)
        even = lax.all_to_all(even, ("half", "y", "core"), split_axis=0, concat_axis=0, tiled=True)
        high, low, kept, sent = gram_call(core, householder, place)
        gram = kept + swap(sent, 1)
        gram = gram + swap(gram, 2)
        scattered = spread(came[0], came[1], kept) + spread(came[2], came[3], gram)
        high = after(high, even)
        current, value, sent, gram = project_call(core, place, even, scattered, high, low, gram, swap(gram, 8))
        value = value + swap(sent, 1)
        value = value + swap(value, 2)
        half = value.shape[0]
        second, third = swap(value, 8), swap(value, 12)
        first = swap(jnp.concatenate([value, gram], axis=0), 4)
        own = jnp.concatenate([(value + first[:half]) + (second + third), gram + first[half:]], axis=0)
        own = own + swap(own, 24)
        other = swap(own, 1)
        return finish_call(core, own, other, tfactors, current, high, low)

    in_specs = (P(("col",) + row, None), P(None, None, row), P())
    out_specs = P("col", row)
    return jax.shard_map(shards, mesh=parts, in_specs=in_specs, out_specs=out_specs, check_vma=False)
```
